128 devices in a mesh: row: 16 (over z, x), col: 8 (over y, core).
Axes of the slice: x: 4, y: 4, z: 4, core: 2. Of those that a mesh axis runs over, the one named last changes fastest.
Arguments:
- density: float32 [16, 80, 128, 128], P('row', 'col'), may hold values from -0.3 to 0.3
- hamiltonian: float32 [16, 80, 128, 128], P('row', 'col'), may hold values from -0.3 to 0.3
- block_rows: int32 [16, 80], P('row', 'col'), may hold values from 0 to 511, as said below
- block_cols: int32 [16, 80], P('row', 'col'), may hold values from 0 to 511, as said below
- left_index: int32 [16, 80, 3], P('row', 'col'), may hold values from -1 to 79, as said below
- right_index: int32 [16, 80, 3], P('row', 'col'), may hold values from -1 to 159, as said below
Outputs:
- new_density: float32 [16, 80, 128, 128], P('row', 'col')
- energy_weighted: float32 [16, 80, 128, 128], P('row', 'col')
The draws below stay inside these ranges and needn't reach their ends.
Inputs may be any that keep to these rules, and one draw needn't show every extreme that they name: -1 marks an empty term and live terms come first in each list; a live term pairs the stored block (i, j) of the left matrix with the stored block (j, k) of the right matrix, where (i, k) is the stored block that it sums into; a list holds all such pairs; a term is live in left_index exactly where it is in right_index; the left block of a live term of device (r, c) is stored on device (r, c - 1), (r, c) or (r, c + 1), column indices counted round. `right_index`: as for left_index. `block_rows`: the block row of a block of device (r, c) leaves the remainder r when divided by 16; the pattern is symmetric, every block row has its diagonal block stored, and the stored blocks of one device are distinct. `block_cols`: a block column k of a block of device (r, c) has (k // 16) % 8 equal to c.
All inputs are finite; a program needn't handle non-finite values.
Results may differ from the reference program's by a relative error of at most 0.0003.
Values sent between devices are 32-bit elements; how exact they have to be, the bound alone decides.
A program may use at most 128 MiB of HBM per device.

```python
import jax
import jax.numpy as jnp
from jax import lax

BS = 128
DIAG = 4
TERMS = 3
SLOTS = 10
GRID_SLOTS = 80
N_ROW = 16
N_COL = 8


def index_of(row_class, col_class, level):
    return row_class % N_ROW + N_ROW * (col_class % N_COL) + N_ROW * N_COL * level


def block_pattern(key):
    base = jax.random.fold_in(key, 31)
    key_perm = jax.random.fold_in(base, 1)
    key_skip = jax.random.fold_in(base, 2)
    key_zero = jax.random.fold_in(base, 3)
    key_pool = jax.random.fold_in(base, 4)
    key_order = jax.random.fold_in(base, 5)
    shift_col = jnp.int32(1)
    next_level = jax.random.permutation(key_perm, DIAG).astype(jnp.int32)
    skipped = jax.random.randint(key_skip, (N_COL,), 0, DIAG).astype(jnp.int32)
    zero_level = ((skipped + jax.random.randint(key_zero, (N_COL,), 1, DIAG)) % DIAG).astype(jnp.int32)
    pool = jax.vmap(lambda one_key: jax.random.permutation(one_key, N_ROW - 1))(jax.random.split(key_pool, N_COL)).astype(jnp.int32) + 1
    levels = jnp.arange(DIAG, dtype=jnp.int32)
    pool_pos = jnp.clip(levels[None, :] - (levels[None, :] > zero_level[:, None]).astype(jnp.int32), 0, N_ROW - 2)
    offsets = jnp.where(levels[None, :] == zero_level[:, None], 0, jnp.take_along_axis(pool, pool_pos, axis=1)).astype(jnp.int32)
    rows_grid = jnp.arange(N_ROW, dtype=jnp.int32)[:, None, None]
    cols_grid = jnp.arange(N_COL, dtype=jnp.int32)[None, :, None]
    diag_ids = jnp.broadcast_to(index_of(rows_grid, cols_grid, levels[None, None, :]), (N_ROW, N_COL, DIAG))
    kept = ((skipped[:, None] + 1 + jnp.arange(DIAG - 1, dtype=jnp.int32)[None, :]) % DIAG).astype(jnp.int32)
    source_col = (jnp.arange(N_COL, dtype=jnp.int32) - shift_col) % N_COL
    fwd_level = kept[source_col]
    fwd_offset = jnp.take_along_axis(offsets[source_col], fwd_level, axis=1)
    fwd_row = index_of(rows_grid, source_col[None, :, None], fwd_level[None])
    fwd_col = index_of(rows_grid + fwd_offset[None], cols_grid, next_level[fwd_level][None])
    rev_offset = jnp.take_along_axis(offsets, kept, axis=1)
    rev_row = index_of(rows_grid, cols_grid + shift_col, next_level[kept][None])
    rev_col = index_of(rows_grid - rev_offset[None], cols_grid, kept[None])
    shape = (N_ROW, N_COL, DIAG - 1)
    all_rows = jnp.concatenate([diag_ids, jnp.broadcast_to(fwd_row, shape), jnp.broadcast_to(rev_row, shape)], axis=2)
    all_cols = jnp.concatenate([diag_ids, jnp.broadcast_to(fwd_col, shape), jnp.broadcast_to(rev_col, shape)], axis=2)
    order = jax.vmap(lambda one_key: jax.random.permutation(one_key, SLOTS))(jax.random.split(key_order, N_ROW * N_COL)).astype(jnp.int32)
    order = order.reshape(N_ROW, N_COL, SLOTS)
    row_ids = jnp.take_along_axis(all_rows, order, axis=2).reshape(N_ROW, N_COL * SLOTS)
    col_ids = jnp.take_along_axis(all_cols, order, axis=2).reshape(N_ROW, N_COL * SLOTS)
    return (row_ids.astype(jnp.int32), col_ids.astype(jnp.int32))


def term_lists(key):
    row_ids, col_ids = block_pattern(key)
    grid_slots = N_COL * SLOTS
    column_len = N_ROW * SLOTS
    right_rows = row_ids.reshape(N_ROW, N_COL, SLOTS).transpose(1, 0, 2).reshape(N_COL, column_len)
    right_cols = col_ids.reshape(N_ROW, N_COL, SLOTS).transpose(1, 0, 2).reshape(N_COL, column_len)
    column_of_slot = jnp.arange(grid_slots, dtype=jnp.int32) // SLOTS
    left_ok = row_ids[:, None, :] == row_ids[:, :, None]
    right_ok = right_cols[column_of_slot][None, :, :] == col_ids[:, :, None]
    inner_ok = col_ids[:, None, :, None] == right_rows[column_of_slot][None, :, None, :]
    matches = left_ok[:, :, :, None] & right_ok[:, :, None, :] & inner_ok
    has_match = jnp.any(matches, axis=3)
    right_of = jnp.sum(jnp.where(matches, jnp.arange(column_len, dtype=jnp.int32), 0), axis=3)
    position = jnp.cumsum(has_match.astype(jnp.int32), axis=2)
    picked_terms = has_match[:, :, None, :] & (position[:, :, None, :] == jnp.arange(1, TERMS + 1, dtype=jnp.int32)[None, None, :, None])
    live_term = jnp.any(picked_terms, axis=3)
    left_list = jnp.where(live_term, jnp.sum(jnp.where(picked_terms, jnp.arange(grid_slots, dtype=jnp.int32), 0), axis=3), -1)
    right_list = jnp.where(live_term, jnp.sum(jnp.where(picked_terms, right_of[:, :, None, :], 0), axis=3), -1)
    return (left_list.astype(jnp.int32), right_list.astype(jnp.int32))


def draw_block_rows(key, part):
    return block_pattern(key)[0]


def draw_block_cols(key, part):
    return block_pattern(key)[1]


def draw_left_index(key, part):
    return term_lists(key)[0]


def draw_right_index(key, part):
    return term_lists(key)[1]


def block_scale(rng, shape, cuts, low, high):
    factor_of = 1.0
    for axis_at, shards_of in cuts:
        draws = jax.random.uniform(jax.random.fold_in(jax.random.fold_in(rng, 6), axis_at), (shards_of,), jnp.float32, low / len(cuts), high / len(cuts))
        factor_of = factor_of * jnp.repeat(jnp.exp(draws), shape[axis_at] // shards_of).reshape((-1,) + (1,) * (len(shape) - 1 - axis_at))
    return factor_of


def scatter_about(rng, shape, spread, most, cuts=(), kind=jnp.bfloat16):
    values = jax.random.normal(rng, shape, jnp.float32) * spread
    if len(cuts) > 0:
        values = block_scale(rng, shape, cuts, -0.22, 0.18) * values
    return jnp.clip(values, min=-most, max=most).astype(kind)


def setup_inputs(seed: int = 0) -> dict:
    streams_of = jax.random.split(jax.random.key(seed), 7)
    density = scatter_about(streams_of[0], (N_ROW, GRID_SLOTS, BS, BS), 0.05, 0.3, ((0, 16), (1, 8)), jnp.float32)
    hamiltonian = scatter_about(streams_of[1], (N_ROW, GRID_SLOTS, BS, BS), 0.05, 0.3, ((0, 16), (1, 8)), jnp.float32)
    block_rows = draw_block_rows(jax.random.fold_in(streams_of[6], 71), 0)
    block_cols = draw_block_cols(jax.random.fold_in(streams_of[6], 71), 0)
    left_index = draw_left_index(jax.random.fold_in(streams_of[6], 71), 0)
    right_index = draw_right_index(jax.random.fold_in(streams_of[6], 71), 0)
    return dict(density=density, hamiltonian=hamiltonian, block_rows=block_rows, block_cols=block_cols, left_index=left_index, right_index=right_index)


def stack_product(row_panel, col_panel, left_part, right_part):
    live_terms = ((left_part >= 0) & (right_part >= 0)).astype(jnp.float32)
    left_blocks = jnp.take(row_panel, jnp.maximum(left_part, 0), axis=0)
    right_blocks = jnp.take(col_panel, jnp.maximum(right_part, 0), axis=0)
    left_blocks = left_blocks * live_terms[:, :, None, None]
    return jnp.einsum("stij,stjk->sik", left_blocks, right_blocks, precision=lax.Precision.HIGHEST)


def grid_product(left_matrix, right_matrix, left_index, right_index):
    def one_row(row_id):
        row_panel = left_matrix[row_id]

        def one_col(col_id):
            offset = (col_id * SLOTS).astype(jnp.int32)
            col_panel = lax.dynamic_slice_in_dim(right_matrix, offset, SLOTS, 1).reshape(N_ROW * SLOTS, BS, BS)
            left_part = lax.dynamic_slice_in_dim(left_index[row_id], offset, SLOTS, 0)
            right_part = lax.dynamic_slice_in_dim(right_index[row_id], offset, SLOTS, 0)
            return stack_product(row_panel, col_panel, left_part, right_part)

        return lax.map(one_col, jnp.arange(N_COL, dtype=jnp.int32)).reshape(N_COL * SLOTS, BS, BS)

    return lax.map(one_row, jnp.arange(N_ROW, dtype=jnp.int32))


def diag_trace(blocks, on_diag):
    return jnp.sum(jnp.where(on_diag, jnp.trace(blocks, axis1=-2, axis2=-1), jnp.float32(0.0)))


def reference(density, hamiltonian, block_rows, block_cols, left_index, right_index):
    on_diag = block_rows == block_cols
    square = grid_product(density, density, left_index, right_index)
    third_power = grid_product(square, density, left_index, right_index)
    fourth = grid_product(square, square, left_index, right_index)
    energy_weighted = grid_product(square, hamiltonian, left_index, right_index)
    trace_one = diag_trace(density, on_diag)
    trace_two = diag_trace(square, on_diag)
    trace_three = diag_trace(third_power, on_diag)
    trace_four = diag_trace(fourth, on_diag)
    trace_f = 4.0 * trace_three - 3.0 * trace_four
    trace_g = trace_four - 2.0 * trace_three + trace_two
    gamma_term = jnp.clip((trace_one - trace_f) / jnp.maximum(jnp.abs(trace_g), 1.0), 0.0, 6.0)
    new_density = 4.0 * third_power - 3.0 * fourth + gamma_term * (fourth - 2.0 * third_power + square)
    return new_density, energy_weighted
```

```python
import jax
import jax.numpy as jnp
from jax import lax
from jax.experimental import pallas as pl
from jax.experimental.pallas import tpu as pltpu
from jax.sharding import PartitionSpec as P

MESH = pl.DeviceIdType.MESH
ROWS = 16
COLS = 8
SLOTS = 10
BS = 128
CUT = BS // ROWS
OTHERS = 2
WANT = SLOTS * OTHERS


def halves(x):
    high = x.astype(jnp.bfloat16)
    low = (x - high.astype(jnp.float32)).astype(jnp.bfloat16)
    return high, low


def left_operand(blocks):
    pairs = [halves(block) for block in blocks]
    parts = [half for pair in pairs for half in pair] + [high for high, _ in pairs]
    return jnp.concatenate(parts, axis=1)


def right_operand(blocks):
    pairs = [halves(block) for block in blocks]
    parts = [high for high, _ in pairs for _ in range(2)] + [low for _, low in pairs]
    return jnp.concatenate(parts, axis=0)


def product(left, right):
    return jnp.dot(left, right, preferred_element_type=jnp.float32)


def kernel(
    d_ref, h_ref, rows_ref, cols_ref, left_ref, right_ref,
    new_ref, ew_ref,
    pan_d, pan_q, own_h, deal_d, deal_h, deal_q, stage, got, mix_base, mix_dir, want_v, want_s, part, part_row, part_col,
    local_sem, near_send, near_recv, deal_send, deal_recv, got_send, got_recv,
    want_send, want_recv, row_send, row_recv, col_send, col_recv,
):
    r, c = lax.axis_index("row"), lax.axis_index("col")
    up, down = lax.rem(c + 1, COLS), lax.rem(c + COLS - 1, COLS)
    first = r * SLOTS
    deal = (deal_d, deal_h, deal_q)
    own_d, own_q = pan_d.at[pl.ds(SLOTS, SLOTS)], pan_q.at[pl.ds(SLOTS, SLOTS)]

    load_d = pltpu.make_async_copy(d_ref, own_d, local_sem.at[0])
    load_h = pltpu.make_async_copy(h_ref, own_h, local_sem.at[1])
    load_d.start()
    load_h.start()

    def row_peer(step):
        return lax.rem(r + step, ROWS)

    def col_peer(step):
        return lax.rem(c + step, COLS)

    barrier = pltpu.get_barrier_semaphore()

    @pl.loop(1, ROWS)
    def _(step):
        pl.semaphore_signal(barrier, inc=1, device_id=(row_peer(step), c), device_id_type=MESH)

    @pl.loop(1, COLS)
    def _(step):
        pl.semaphore_signal(barrier, inc=1, device_id=(r, col_peer(step)), device_id_type=MESH)

    lane = lax.broadcasted_iota(jnp.int32, (1, BS), 1)
    wanted = jnp.zeros((1, BS), jnp.int32)
    for s in range(SLOTS):
        own = first + s
        one, two, three = right_ref[s, 0], right_ref[s, 1], right_ref[s, 2]
        u0 = jnp.maximum(jnp.where(one == own, two, one), 0)
        u1 = jnp.maximum(jnp.where(three == own, two, three), 0)
        wanted = jnp.where(lane == 2 * s, u0, jnp.where(lane == 2 * s + 1, u1, wanted))
    want_v[r] = wanted

    zero_block = jnp.zeros((BS, BS), jnp.float32)
    pan_d[3 * SLOTS] = zero_block
    pan_q[3 * SLOTS] = zero_block

    pl.semaphore_wait(barrier, ROWS + COLS - 2)

    def want_copy(src, dst, peer):
        return pltpu.make_async_remote_copy(
            src_ref=want_v.at[src], dst_ref=want_v.at[src], send_sem=want_send.at[dst], recv_sem=want_recv.at[src],
            device_id=(peer, c), device_id_type=MESH,
        )

    def deal_copy(k, own, src, dst, peer):
        return pltpu.make_async_remote_copy(
            src_ref=own.at[:, pl.ds(pl.multiple_of(dst * CUT, CUT), CUT), :],
            dst_ref=deal[k].at[pl.ds(src * SLOTS, SLOTS)],
            send_sem=deal_send.at[k, dst], recv_sem=deal_recv.at[k, src],
            device_id=(peer, c), device_id_type=MESH,
        )

    def got_copy(k, src, dst, peer):
        return pltpu.make_async_remote_copy(
            src_ref=stage.at[k, dst], dst_ref=got.at[k, src],
            send_sem=got_send.at[k, dst], recv_sem=got_recv.at[k, src],
            device_id=(peer, c), device_id_type=MESH,
        )

    def near_copies(k, own, pan):
        to_up = pltpu.make_async_remote_copy(
            src_ref=own, dst_ref=pan.at[pl.ds(0, SLOTS)],
            send_sem=near_send.at[k, 0], recv_sem=near_recv.at[k, 0],
            device_id=(r, up), device_id_type=MESH,
        )
        to_down = pltpu.make_async_remote_copy(
            src_ref=own, dst_ref=pan.at[pl.ds(2 * SLOTS, SLOTS)],
            send_sem=near_send.at[k, 1], recv_sem=near_recv.at[k, 1],
            device_id=(r, down), device_id_type=MESH,
        )
        return to_up, to_down

    def deal_out(k, own):
        @pl.loop(1, ROWS)
        def _(step):
            dst = row_peer(step)
            deal_copy(k, own, r, dst, dst).start()

        mine = pl.ds(pl.multiple_of(r * CUT, CUT), CUT)
        for s in range(SLOTS):
            deal[k][first + s] = own[s, mine, :]

    def deal_in(k, own):
        @pl.loop(1, ROWS)
        def _(step):
            src = row_peer(step)
            deal_copy(k, own, src, r, src).wait_recv()

    def pass_on(k):
        @pl.loop(1, ROWS)
        def _(step):
            dst = row_peer(step)
            for q in range(WANT):
                stage[k, dst, q] = deal[k][want_s[dst, 0, q]]
            got_copy(k, r, dst, dst).start()

        for q in range(WANT):
            got[k, r, q] = deal[k][want_s[r, 0, q]]

    def get_in(k):
        @pl.loop(1, ROWS)
        def _(step):
            src = row_peer(step)
            got_copy(k, src, r, src).wait_recv()

    def fetched(k, place):
        return got[k, :, place].reshape(BS, BS)

    def left_blocks(pan, s):
        own = first + s
        places = []
        for t in range(3):
            index = left_ref[s, t]
            held = jnp.maximum(index, 0)
            owner = lax.div(held, SLOTS)
            within = held - owner * SLOTS
            near = lax.rem(owner - c + 1 + COLS, COLS)
            places.append(jnp.where(index >= 0, jnp.minimum(near * SLOTS + within, 3 * SLOTS), 3 * SLOTS))
        first_is, second_is, third_is = (right_ref[s, t] == own for t in range(3))
        self_place = jnp.where(first_is, places[0], jnp.where(second_is, places[1], places[2]))
        u0 = jnp.where(first_is, places[1], places[0])
        u1 = jnp.where(third_is, places[1], places[2])
        return [pan[self_place], pan[u0], pan[u1]]

    load_d.wait()
    near_d = near_copies(0, own_d, pan_d)

    @pl.loop(1, ROWS)
    def _(step):
        dst = row_peer(step)
        want_copy(r, dst, dst).start()

    deal_out(0, own_d)
    for copy in near_d:
        copy.start()
    load_h.wait()
    deal_out(1, own_h)

    @pl.loop(1, ROWS)
    def _(step):
        src = row_peer(step)
        want_copy(src, r, src).wait_recv()

    to_smem = pltpu.make_async_copy(want_v, want_s, local_sem.at[2])
    to_smem.start()
    to_smem.wait()

    deal_in(0, own_d)
    pass_on(0)
    deal_in(1, own_h)
    pass_on(1)
    for copy in near_d:
        copy.wait_recv()
    get_in(0)

    eye = lax.broadcasted_iota(jnp.int32, (BS, BS), 0) == lax.broadcasted_iota(jnp.int32, (BS, BS), 1)

    def trace_row(block, s):
        on = (rows_ref[0, s] == cols_ref[0, s]).astype(jnp.float32)
        return jnp.sum(jnp.where(eye, block, 0.0), axis=0, keepdims=True) * on

    part[...] = jnp.zeros_like(part)

    @pl.loop(0, SLOTS)
    def _(s):
        own = pan_d[SLOTS + s]
        right = right_operand([own, fetched(0, 2 * s), fetched(0, 2 * s + 1)])
        square = product(left_operand(left_blocks(pan_d, s)), right)
        pan_q[SLOTS + s] = square
        part[0:1, :] += trace_row(own, s)
        part[1:2, :] += trace_row(square, s)

    near_q = near_copies(1, own_q, pan_q)
    deal_out(2, own_q)
    for copy in near_q:
        copy.start()
    deal_in(2, own_q)
    pass_on(2)
    for copy in near_q:
        copy.wait_recv()
    get_in(2)

    @pl.loop(0, SLOTS)
    def _(s):
        left = left_operand(left_blocks(pan_q, s))
        square = pan_q[SLOTS + s]
        right_d = right_operand([pan_d[SLOTS + s], fetched(0, 2 * s), fetched(0, 2 * s + 1)])
        right_q = right_operand([square, fetched(2, 2 * s), fetched(2, 2 * s + 1)])
        both = product(left, jnp.concatenate([right_d, right_q], axis=1))
        cube, fourth = both[:, :BS], both[:, BS:]
        mix_base[s] = 4.0 * cube - 3.0 * fourth
        mix_dir[s] = fourth - 2.0 * cube + square
        part[2:3, :] += trace_row(cube, s)
        part[3:4, :] += trace_row(fourth, s)

    def row_copy(src, dst, peer):
        return pltpu.make_async_remote_copy(
            src_ref=part, dst_ref=part_row.at[src], send_sem=row_send.at[dst], recv_sem=row_recv.at[src],
            device_id=(peer, c), device_id_type=MESH,
        )

    def col_copy(src, dst, peer):
        return pltpu.make_async_remote_copy(
            src_ref=part_col.at[src], dst_ref=part_col.at[src], send_sem=col_send.at[dst], recv_sem=col_recv.at[src],
            device_id=(r, peer), device_id_type=MESH,
        )

    @pl.loop(1, ROWS)
    def _(step):
        dst = row_peer(step)
        row_copy(r, dst, dst).start()

    part_row[r] = part[...]
    get_in(1)

    @pl.loop(0, SLOTS)
    def _(s):
        right = right_operand([own_h[s], fetched(1, 2 * s), fetched(1, 2 * s + 1)])
        ew_ref[s] = product(left_operand(left_blocks(pan_q, s)), right)

    @pl.loop(1, ROWS)
    def _(step):
        src = row_peer(step)
        row_copy(src, r, src).wait_recv()

    part_col[c] = jnp.sum(part_row[...], axis=0)

    @pl.loop(1, COLS)
    def _(step):
        dst = col_peer(step)
        col_copy(c, dst, dst).start()

    @pl.loop(1, COLS)
    def _(step):
        src = col_peer(step)
        col_copy(src, c, src).wait_recv()

    traces = jnp.sum(jnp.sum(part_col[...], axis=0), axis=1, keepdims=True)
    one, two, three, four = (traces[k : k + 1, :] for k in range(4))
    trace_f = 4.0 * three - 3.0 * four
    trace_g = four - 2.0 * three + two
    gamma = jnp.clip((one - trace_f) / jnp.maximum(jnp.abs(trace_g), 1.0), 0.0, 6.0)

    @pl.loop(0, SLOTS)
    def _(s):
        new_ref[s] = mix_base[s] + gamma * mix_dir[s]

    for copy in (*near_d, *near_q):
        copy.wait_send()

    @pl.loop(1, ROWS)
    def _(step):
        dst = row_peer(step)
        want_copy(r, dst, dst).wait_send()
        row_copy(r, dst, dst).wait_send()
        for k, own in enumerate((own_d, own_h, own_q)):
            deal_copy(k, own, r, dst, dst).wait_send()
            got_copy(k, r, dst, dst).wait_send()

    @pl.loop(1, COLS)
    def _(step):
        dst = col_peer(step)
        col_copy(c, dst, dst).wait_send()


def shards(density, hamiltonian, block_rows, block_cols, left_index, right_index):
    any_space = pl.BlockSpec(memory_space=pl.ANY)
    smem = pl.BlockSpec(memory_space=pltpu.SMEM)
    vmem = pl.BlockSpec(memory_space=pltpu.VMEM)
    block = jax.ShapeDtypeStruct((SLOTS, BS, BS), jnp.float32)
    dma = pltpu.SemaphoreType.DMA
    new, ew = pl.pallas_call(
        kernel,
        out_shape=(block, block),
        in_specs=[any_space, any_space, smem, smem, smem, smem],
        out_specs=(vmem, vmem),
        scratch_shapes=[
            pltpu.VMEM((3 * SLOTS + 1, BS, BS), jnp.float32),
            pltpu.VMEM((3 * SLOTS + 1, BS, BS), jnp.float32),
            pltpu.VMEM((SLOTS, BS, BS), jnp.float32),
            pltpu.VMEM((ROWS * SLOTS, CUT, BS), jnp.float32),
            pltpu.VMEM((ROWS * SLOTS, CUT, BS), jnp.float32),
            pltpu.VMEM((ROWS * SLOTS, CUT, BS), jnp.float32),
            pltpu.VMEM((3, ROWS, WANT, CUT, BS), jnp.float32),
            pltpu.VMEM((3, ROWS, WANT, CUT, BS), jnp.float32),
            pltpu.VMEM((SLOTS, BS, BS), jnp.float32),
            pltpu.VMEM((SLOTS, BS, BS), jnp.float32),
            pltpu.VMEM((ROWS, 1, BS), jnp.int32),
            pltpu.SMEM((ROWS, 1, BS), jnp.int32),
            pltpu.VMEM((8, BS), jnp.float32),
            pltpu.VMEM((ROWS, 8, BS), jnp.float32),
            pltpu.VMEM((COLS, 8, BS), jnp.float32),
            dma((3,)),
            dma((2, 2)),
            dma((2, 2)),
            dma((3, ROWS)),
            dma((3, ROWS)),
            dma((3, ROWS)),
            dma((3, ROWS)),
            dma((ROWS,)),
            dma((ROWS,)),
            dma((ROWS,)),
            dma((ROWS,)),
            dma((COLS,)),
            dma((COLS,)),
        ],
        compiler_params=pltpu.CompilerParams(
            collective_id=0, has_side_effects=True, vmem_limit_bytes=40 * 1024 * 1024
        ),
        cost_estimate=pl.CostEstimate(flops=2 * 9 * 4 * SLOTS * BS**3, bytes_accessed=5 * SLOTS * BS * BS, transcendentals=0),
    )(density[0], hamiltonian[0], block_rows, block_cols, left_index[0], right_index[0])
    return new[None], ew[None]


def solution(mesh):
    in_specs = (
        P("row", "col", None, None),
        P("row", "col", None, None),
        P("row", "col"),
        P("row", "col"),
        P("row", "col", None),
        P("row", "col", None),
    )
    out_specs = (P("row", "col", None, None), P("row", "col", None, None))
    return jax.shard_map(shards, mesh=mesh, in_specs=in_specs, out_specs=out_specs, check_vma=False)
```

```python
import functools

import jax
import jax.numpy as jnp
from jax import lax
from jax.experimental import pallas as pl
from jax.experimental.pallas import tpu as pltpu
from jax.sharding import PartitionSpec as P

MESH = pl.DeviceIdType.MESH
ROWS = 16
COLS = 8
SLOTS = 10
BS = 128
CUT = BS // ROWS
OTHERS = 2
WANT_MOST = SLOTS * OTHERS
WANT_FEW = 8


def halves(x):
    high = x.astype(jnp.bfloat16)
    low = (x - high.astype(jnp.float32)).astype(jnp.bfloat16)
    return high, low


def left_operand(blocks):
    pairs = [halves(block) for block in blocks]
    parts = [half for pair in pairs for half in pair] + [high for high, _ in pairs]
    return jnp.concatenate(parts, axis=1)


def right_operand(blocks):
    pairs = [halves(block) for block in blocks]
    parts = [high for high, _ in pairs for _ in range(2)] + [low for _, low in pairs]
    return jnp.concatenate(parts, axis=0)


def product(left, right):
    return jnp.dot(left, right, preferred_element_type=jnp.float32)


def kernel(
    cap,
    d_ref, h_ref, rows_ref, cols_ref, left_ref, right_ref,
    new_ref, ew_ref, over_ref,
    pan_d, pan_q, own_h, deal_d, deal_h, deal_q, stage, got_d, got_h, got_q, mix_base, mix_dir, new_v, ew_v,
    rows_s, cols_s, left_s, right_s, place_s, want_v, want_s, part, part_row, part_col,
    local_sem, near_send, near_recv, deal_send, deal_recv, got_send, got_recv,
    want_send, want_recv, row_send, row_recv, col_send, col_recv,
):
    r, c = lax.axis_index("row"), lax.axis_index("col")
    up, down = lax.rem(c + 1, COLS), lax.rem(c + COLS - 1, COLS)
    first = r * SLOTS
    deal, got = (deal_d, deal_h, deal_q), (got_d, got_h, got_q)
    own_d, own_q = pan_d.at[pl.ds(SLOTS, SLOTS)], pan_q.at[pl.ds(SLOTS, SLOTS)]

    def row_peer(step):
        return lax.rem(r + step, ROWS)

    def col_peer(step):
        return lax.rem(c + step, COLS)

    barrier = pltpu.get_barrier_semaphore()

    @pl.loop(1, ROWS)
    def _(step):
        pl.semaphore_signal(barrier, inc=1, device_id=(row_peer(step), c), device_id_type=MESH)

    @pl.loop(1, COLS)
    def _(step):
        pl.semaphore_signal(barrier, inc=1, device_id=(r, col_peer(step)), device_id_type=MESH)

    loads = [
        pltpu.make_async_copy(src, dst, local_sem.at[k])
        for k, (src, dst) in enumerate(
            (
                (right_ref, right_s),
                (d_ref, own_d),
                (left_ref, left_s),
                (h_ref, own_h),
                (rows_ref, rows_s),
                (cols_ref, cols_s),
            )
        )
    ]
    for load in loads:
        load.start()
    loads[0].wait()

    lane = lax.broadcasted_iota(jnp.int32, (1, BS), 1)
    wanted = jnp.zeros((1, BS), jnp.int32)
    count = jnp.int32(0)
    for s in range(SLOTS):
        own = first + s
        one, two, three = (right_s[t, 0, s] for t in range(3))
        for u, index in enumerate((jnp.where(one == own, two, one), jnp.where(three == own, two, three))):
            live = index >= 0
            near = index - first
            here = jnp.logical_and(near >= 0, near < SLOTS)
            away = jnp.logical_and(live, jnp.logical_not(here))
            place_s[2 * s + u] = jnp.where(away, jnp.minimum(count, cap - 1), jnp.where(here, cap + near, 0))
            wanted = jnp.where(lane == jnp.where(away, count, -1), index, wanted)
            count = count + away.astype(jnp.int32)
    want_v[r] = wanted
    over = jnp.where(count > cap, 1.0, 0.0)

    zero_block = jnp.zeros((BS, BS), jnp.float32)
    pan_d[3 * SLOTS] = zero_block
    pan_q[3 * SLOTS] = zero_block
    loads[1].wait()

    pl.semaphore_wait(barrier, ROWS + COLS - 2)

    def want_copy(src, dst, peer):
        return pltpu.make_async_remote_copy(
            src_ref=want_v.at[src], dst_ref=want_v.at[src], send_sem=want_send.at[dst], recv_sem=want_recv.at[src],
            device_id=(peer, c), device_id_type=MESH,
        )

    def deal_copy(k, own, src, dst, peer):
        return pltpu.make_async_remote_copy(
            src_ref=own.at[:, pl.ds(pl.multiple_of(dst * CUT, CUT), CUT), :],
            dst_ref=deal[k].at[pl.ds(src * SLOTS, SLOTS)],
            send_sem=deal_send.at[k, dst], recv_sem=deal_recv.at[k, src],
            device_id=(peer, c), device_id_type=MESH,
        )

    def got_copy(k, src, dst, peer):
        return pltpu.make_async_remote_copy(
            src_ref=stage.at[k, dst], dst_ref=got[k].at[src, pl.ds(0, cap)],
            send_sem=got_send.at[k, dst], recv_sem=got_recv.at[k, src],
            device_id=(peer, c), device_id_type=MESH,
        )

    def near_copies(k, own, pan):
        to_up = pltpu.make_async_remote_copy(
            src_ref=own, dst_ref=pan.at[pl.ds(0, SLOTS)],
            send_sem=near_send.at[k, 0], recv_sem=near_recv.at[k, 0],
            device_id=(r, up), device_id_type=MESH,
        )
        to_down = pltpu.make_async_remote_copy(
            src_ref=own, dst_ref=pan.at[pl.ds(2 * SLOTS, SLOTS)],
            send_sem=near_send.at[k, 1], recv_sem=near_recv.at[k, 1],
            device_id=(r, down), device_id_type=MESH,
        )
        return to_up, to_down

    def deal_out(k, own):
        @pl.loop(1, ROWS)
        def _(step):
            dst = row_peer(step)
            deal_copy(k, own, r, dst, dst).start()

        mine = pl.ds(pl.multiple_of(r * CUT, CUT), CUT)
        for s in range(SLOTS):
            deal[k][first + s] = own[s, mine, :]
            got[k][:, cap + s] = own[s].reshape(ROWS, CUT, BS)

    def deal_in(k, own):
        @pl.loop(1, ROWS)
        def _(step):
            src = row_peer(step)
            deal_copy(k, own, src, r, src).wait_recv()

    def pick(k, dst, q):
        return deal[k][want_s[dst, 0, q]]

    def pass_on(k):
        @pl.loop(1, ROWS)
        def _(step):
            dst = row_peer(step)
            for q in range(cap):
                stage[k, dst, q] = pick(k, dst, q)
            got_copy(k, r, dst, dst).start()

        for q in range(cap):
            got[k][r, q] = pick(k, r, q)

    def get_in(k):
        @pl.loop(1, ROWS)
        def _(step):
            src = row_peer(step)
            got_copy(k, src, r, src).wait_recv()

    def right_blocks(k, s):
        places = (cap + s, place_s[2 * s], place_s[2 * s + 1])
        return right_operand([got[k][:, place].reshape(BS, BS) for place in places])

    def left_blocks(pan, s):
        own = first + s
        places = []
        for t in range(3):
            index = left_s[t, 0, s]
            held = jnp.maximum(index, 0)
            owner = lax.div(held, SLOTS)
            within = held - owner * SLOTS
            near = lax.rem(owner - c + 1 + COLS, COLS)
            place = jnp.minimum(near * SLOTS + within, 3 * SLOTS)
            places.append(jnp.where(index >= 0, place, 3 * SLOTS))
        first_is, second_is, third_is = (right_s[t, 0, s] == own for t in range(3))
        self_place = jnp.where(first_is, places[0], jnp.where(second_is, places[1], places[2]))
        u0 = jnp.where(first_is, places[1], places[0])
        u1 = jnp.where(third_is, places[1], places[2])
        return left_operand([pan[self_place], pan[u0], pan[u1]])

    @pl.loop(1, ROWS)
    def _(step):
        dst = row_peer(step)
        want_copy(r, dst, dst).start()

    near_d = near_copies(0, own_d, pan_d)
    deal_out(0, own_d)
    for copy in near_d:
        copy.start()

    @pl.loop(1, ROWS)
    def _(step):
        src = row_peer(step)
        want_copy(src, r, src).wait_recv()

    to_smem = pltpu.make_async_copy(want_v, want_s, local_sem.at[6])
    to_smem.start()
    for load in loads[2:]:
        load.wait()
    to_smem.wait()

    deal_in(0, own_d)
    pass_on(0)
    deal_out(1, own_h)
    for copy in near_d:
        copy.wait_recv()
    get_in(0)

    eye = lax.broadcasted_iota(jnp.int32, (BS, BS), 0) == lax.broadcasted_iota(jnp.int32, (BS, BS), 1)

    def trace_row(block, s):
        on = (rows_s[0, s] == cols_s[0, s]).astype(jnp.float32)
        return jnp.sum(jnp.where(eye, block, 0.0), axis=0, keepdims=True) * on

    part[...] = jnp.zeros_like(part)

    @pl.loop(0, SLOTS)
    def _(s):
        square = product(left_blocks(pan_d, s), right_blocks(0, s))
        pan_q[SLOTS + s] = square
        part[0:1, :] += trace_row(pan_d[SLOTS + s], s)
        part[1:2, :] += trace_row(square, s)

    near_q = near_copies(1, own_q, pan_q)
    deal_out(2, own_q)
    for copy in near_q:
        copy.start()
    deal_in(1, own_h)
    deal_in(2, own_q)
    pass_on(2)
    pass_on(1)
    for copy in near_q:
        copy.wait_recv()
    get_in(2)

    @pl.loop(0, SLOTS)
    def _(s):
        square = pan_q[SLOTS + s]
        both = product(left_blocks(pan_q, s), jnp.concatenate([right_blocks(0, s), right_blocks(2, s)], axis=1))
        cube, fourth = both[:, :BS], both[:, BS:]
        mix_base[s] = 4.0 * cube - 3.0 * fourth
        mix_dir[s] = fourth - 2.0 * cube + square
        part[2:3, :] += trace_row(cube, s)
        part[3:4, :] += trace_row(fourth, s)

    part[4:5, :] = jnp.zeros((1, BS), jnp.float32) + over

    def row_copy(src, dst, peer):
        return pltpu.make_async_remote_copy(
            src_ref=part, dst_ref=part_row.at[src], send_sem=row_send.at[dst], recv_sem=row_recv.at[src],
            device_id=(peer, c), device_id_type=MESH,
        )

    def col_copy(src, dst, peer):
        return pltpu.make_async_remote_copy(
            src_ref=part_col.at[src], dst_ref=part_col.at[src], send_sem=col_send.at[dst], recv_sem=col_recv.at[src],
            device_id=(r, peer), device_id_type=MESH,
        )

    @pl.loop(1, ROWS)
    def _(step):
        dst = row_peer(step)
        row_copy(r, dst, dst).start()

    part_row[r] = part[...]

    @pl.loop(1, ROWS)
    def _(step):
        src = row_peer(step)
        row_copy(src, r, src).wait_recv()

    part_col[c] = jnp.sum(part_row[...], axis=0)

    @pl.loop(1, COLS)
    def _(step):
        dst = col_peer(step)
        col_copy(c, dst, dst).start()

    get_in(1)

    @pl.loop(0, SLOTS)
    def _(s):
        ew_v[s] = product(left_blocks(pan_q, s), right_blocks(1, s))

    put_ew = pltpu.make_async_copy(ew_v, ew_ref, local_sem.at[7])
    put_ew.start()

    @pl.loop(1, COLS)
    def _(step):
        src = col_peer(step)
        col_copy(src, c, src).wait_recv()

    sums = jnp.sum(part_col[...], axis=0)
    over_ref[0, 0] = jnp.sum(sums[4:5, :])
    traces = jnp.sum(sums, axis=1, keepdims=True)
    one, two, three, four = (traces[k : k + 1, :] for k in range(4))
    trace_f = 4.0 * three - 3.0 * four
    trace_g = four - 2.0 * three + two
    gamma = jnp.clip((one - trace_f) / jnp.maximum(jnp.abs(trace_g), 1.0), 0.0, 6.0)

    @pl.loop(0, SLOTS)
    def _(s):
        new_v[s] = mix_base[s] + gamma * mix_dir[s]

    put_new = pltpu.make_async_copy(new_v, new_ref, local_sem.at[8])
    put_new.start()

    for copy in (*near_d, *near_q):
        copy.wait_send()

    @pl.loop(1, ROWS)
    def _(step):
        dst = row_peer(step)
        want_copy(r, dst, dst).wait_send()
        row_copy(r, dst, dst).wait_send()
        for k, own in enumerate((own_d, own_h, own_q)):
            deal_copy(k, own, r, dst, dst).wait_send()
            got_copy(k, r, dst, dst).wait_send()

    @pl.loop(1, COLS)
    def _(step):
        dst = col_peer(step)
        col_copy(c, dst, dst).wait_send()

    put_ew.wait()
    put_new.wait()


def step(cap, collective_id, *operands):
    any_space = pl.BlockSpec(memory_space=pl.ANY)
    smem = pl.BlockSpec(memory_space=pltpu.SMEM)
    block = jax.ShapeDtypeStruct((SLOTS, BS, BS), jnp.float32)
    dma = pltpu.SemaphoreType.DMA
    panel = pltpu.VMEM((3 * SLOTS + 1, BS, BS), jnp.float32)
    own = pltpu.VMEM((SLOTS, BS, BS), jnp.float32)
    dealt = pltpu.VMEM((ROWS * SLOTS, CUT, BS), jnp.float32)
    fetched = pltpu.VMEM((ROWS, cap + SLOTS, CUT, BS), jnp.float32)
    return pl.pallas_call(
        functools.partial(kernel, cap),
        out_shape=(block, block, jax.ShapeDtypeStruct((1, 1), jnp.float32)),
        in_specs=[any_space] * 6,
        out_specs=(any_space, any_space, smem),
        scratch_shapes=[
            panel,
            panel,
            own,
            dealt,
            dealt,
            dealt,
            pltpu.VMEM((3, ROWS, cap, CUT, BS), jnp.float32),
            fetched,
            fetched,
            fetched,
            own,
            own,
            own,
            own,
            pltpu.SMEM((1, SLOTS), jnp.int32),
            pltpu.SMEM((1, SLOTS), jnp.int32),
            pltpu.SMEM((3, 1, SLOTS), jnp.int32),
            pltpu.SMEM((3, 1, SLOTS), jnp.int32),
            pltpu.SMEM((WANT_MOST,), jnp.int32),
            pltpu.VMEM((ROWS, 1, BS), jnp.int32),
            pltpu.SMEM((ROWS, 1, BS), jnp.int32),
            pltpu.VMEM((8, BS), jnp.float32),
            pltpu.VMEM((ROWS, 8, BS), jnp.float32),
            pltpu.VMEM((COLS, 8, BS), jnp.float32),
            dma((9,)),
            dma((2, 2)),
            dma((2, 2)),
            dma((3, ROWS)),
            dma((3, ROWS)),
            dma((3, ROWS)),
            dma((3, ROWS)),
            dma((ROWS,)),
            dma((ROWS,)),
            dma((ROWS,)),
            dma((ROWS,)),
            dma((COLS,)),
            dma((COLS,)),
        ],
        compiler_params=pltpu.CompilerParams(
            collective_id=collective_id, has_side_effects=True, vmem_limit_bytes=60 * 1024 * 1024
        ),
        cost_estimate=pl.CostEstimate(flops=2 * 9 * 4 * SLOTS * BS**3, bytes_accessed=5 * SLOTS * BS * BS, transcendentals=0),
    )(*operands)


def shards(density, hamiltonian, block_rows, block_cols, left_index, right_index):
    terms_first = (2, 0, 1)
    operands = (
        density[0], hamiltonian[0], block_rows, block_cols,
        jnp.transpose(left_index, terms_first), jnp.transpose(right_index, terms_first),
    )
    new, ew, over = step(WANT_FEW, 0, *operands)
    new, ew = lax.cond(
        over[0, 0] > 0.0,
        lambda new, ew, *operands: tuple(step(WANT_MOST, 1, *operands)[:2]),
        lambda new, ew, *operands: (new, ew),
        new, ew, *operands,
    )
    return new[None], ew[None]


def solution(mesh):
    in_specs = (
        P("row", "col", None, None),
        P("row", "col", None, None),
        P("row", "col"),
        P("row", "col"),
        P("row", "col", None),
        P("row", "col", None),
    )
    out_specs = (P("row", "col", None, None), P("row", "col", None, None))
    return jax.shard_map(shards, mesh=mesh, in_specs=in_specs, out_specs=out_specs, check_vma=False)
```

```python
import functools

import jax
import jax.numpy as jnp
from jax import lax
from jax.experimental import pallas as pl
from jax.experimental.pallas import tpu as pltpu
from jax.sharding import PartitionSpec as P

MESH = pl.DeviceIdType.MESH
ROWS = 16
COLS = 8
SLOTS = 10
BS = 128
CUT = BS // ROWS
OTHERS = 2
WANT_MOST = SLOTS * OTHERS
WANT_FEW = 8
OFF_DIAG = 6
TARGET = 32
PLACES = 64


def halves(x):
    high = x.astype(jnp.bfloat16)
    low = (x - high.astype(jnp.float32)).astype(jnp.bfloat16)
    return high, low


def left_operand(blocks):
    pairs = [halves(block) for block in blocks]
    parts = [half for pair in pairs for half in pair] + [high for high, _ in pairs]
    return jnp.concatenate(parts, axis=1)


def right_operand(blocks):
    pairs = [halves(block) for block in blocks]
    parts = [high for high, _ in pairs for _ in range(2)] + [low for _, low in pairs]
    return jnp.concatenate(parts, axis=0)


def product(left, right):
    return jnp.dot(left, right, preferred_element_type=jnp.float32)


def kernel(
    cap, dealt,
    d_ref, h_ref, left_ref, right_ref,
    new_ref, ew_ref, over_ref,
    pan_d, pan_q, own_d, own_h, own_q, pack, deal_d, deal_h, deal_q, stage, got_d, got_h, got_q, mix_base, mix_dir, new_v, ew_v,
    mirror_stage, mirror_in, left_s, right_s, place_s, table_v, table_s, want_v, want_s, part, part_row, part_col,
    local_sem, near_send, near_recv, deal_send, deal_recv, got_send, got_recv,
    want_send, want_recv, row_send, row_recv, col_send, col_recv, table_send, table_recv, mirror_send, mirror_recv,
):
    r, c = lax.axis_index("row"), lax.axis_index("col")
    up, down = lax.rem(c + 1, COLS), lax.rem(c + COLS - 1, COLS)
    first = r * SLOTS
    deal, got = (deal_d, deal_h, deal_q), (got_d, got_h, got_q)
    middle = pl.ds(SLOTS, SLOTS)

    def row_peer(step):
        return lax.rem(r + step, ROWS)

    def col_peer(step):
        return lax.rem(c + step, COLS)

    loads = [
        pltpu.make_async_copy(src, dst, local_sem.at[k])
        for k, (src, dst) in enumerate(
            (
                (right_ref, right_s),
                (d_ref, own_d),
                (d_ref, pan_d.at[middle]),
                (left_ref, left_s),
                (h_ref, own_h),
            )
        )
    ]
    for load in loads:
        load.start()

    barrier = pltpu.get_barrier_semaphore()

    @pl.loop(1, ROWS)
    def _(step):
        pl.semaphore_signal(barrier, inc=1, device_id=(row_peer(step), c), device_id_type=MESH)

    @pl.loop(1, COLS)
    def _(step):
        pl.semaphore_signal(barrier, inc=1, device_id=(r, col_peer(step)), device_id_type=MESH)

    loads[0].wait()

    lane = lax.broadcasted_iota(jnp.int32, (1, BS), 1)
    wanted = jnp.full((1, BS), PLACES, jnp.int32)
    count, packed = jnp.int32(0), jnp.int32(0)
    slots = [jnp.int32(p) for p in range(dealt)]
    for s in range(SLOTS):
        own = first + s
        one, two, three = (right_s[t, 0, s] for t in range(3))
        lone = True
        for u, index in enumerate((jnp.where(one == own, two, one), jnp.where(three == own, two, three))):
            live = index >= 0
            near = index - first
            here = jnp.logical_and(near >= 0, near < SLOTS)
            away = jnp.logical_and(live, jnp.logical_not(here))
            lone = jnp.logical_and(lone, jnp.logical_not(away))
            place_s[2 * s + u] = jnp.where(away, jnp.minimum(count, cap - 1), jnp.where(here, cap + near, 0))
            held = jnp.maximum(index, 0)
            owner = lax.div(held, SLOTS)
            address = owner * BS + PLACES + held - owner * SLOTS
            wanted = jnp.where(lane == jnp.where(away, count, -1), address, wanted)
            count = count + away.astype(jnp.int32)
        if dealt == SLOTS:
            wanted = jnp.where(lane == PLACES + s, r * dealt + s, wanted)
        else:
            wanted = jnp.where(lane == PLACES + s, r * dealt + jnp.minimum(packed, dealt - 1), wanted)
            here = jnp.where(lone, -1, packed)
            for p in range(min(s + 1, dealt)):
                slots[p] = jnp.where(here == p, s, slots[p])
            packed = packed + jnp.logical_not(lone).astype(jnp.int32)
    want_v[r] = wanted
    over = jnp.where(count > cap, 1.0, 0.0)

    zero_block = jnp.zeros((BS, BS), jnp.float32)
    pan_d[3 * SLOTS] = zero_block
    pan_q[3 * SLOTS] = zero_block
    loads[1].wait()

    pl.semaphore_wait(barrier, ROWS + COLS - 2)

    def want_copy(src, dst, peer):
        return pltpu.make_async_remote_copy(
            src_ref=want_v.at[src], dst_ref=want_v.at[src], send_sem=want_send.at[dst], recv_sem=want_recv.at[src],
            device_id=(peer, c), device_id_type=MESH,
        )

    def deal_copy(k, src, dst, peer):
        return pltpu.make_async_remote_copy(
            src_ref=pack.at[k, :, pl.ds(pl.multiple_of(dst * CUT, CUT), CUT), :],
            dst_ref=deal[k].at[pl.ds(src * dealt, dealt)],
            send_sem=deal_send.at[k, dst], recv_sem=deal_recv.at[k, src],
            device_id=(peer, c), device_id_type=MESH,
        )

    def got_copy(k, src, dst, peer):
        return pltpu.make_async_remote_copy(
            src_ref=stage.at[k, dst], dst_ref=got[k].at[src, pl.ds(0, cap)],
            send_sem=got_send.at[k, dst], recv_sem=got_recv.at[k, src],
            device_id=(peer, c), device_id_type=MESH,
        )

    def near_copies(k, own, pan):
        to_up = pltpu.make_async_remote_copy(
            src_ref=own, dst_ref=pan.at[pl.ds(0, SLOTS)],
            send_sem=near_send.at[k, 0], recv_sem=near_recv.at[k, 0],
            device_id=(r, up), device_id_type=MESH,
        )
        to_down = pltpu.make_async_remote_copy(
            src_ref=own, dst_ref=pan.at[pl.ds(2 * SLOTS, SLOTS)],
            send_sem=near_send.at[k, 1], recv_sem=near_recv.at[k, 1],
            device_id=(r, down), device_id_type=MESH,
        )
        return to_up, to_down

    table_copies = [
        pltpu.make_async_remote_copy(
            src_ref=table_v.at[2], dst_ref=table_v.at[k], send_sem=table_send.at[k], recv_sem=table_recv.at[k],
            device_id=(r, peer), device_id_type=MESH,
        )
        for k, peer in enumerate((up, down))
    ]
    mirror_copies = [
        pltpu.make_async_remote_copy(
            src_ref=mirror_stage.at[k], dst_ref=mirror_in.at[pl.ds(k * OFF_DIAG, OFF_DIAG)],
            send_sem=mirror_send.at[k], recv_sem=mirror_recv.at[k],
            device_id=(r, peer), device_id_type=MESH,
        )
        for k, peer in enumerate((up, down))
    ]

    def deal_out(k, own):
        for p in range(dealt):
            pack[k, p] = own[slots[p]]

        @pl.loop(1, ROWS)
        def _(step):
            dst = row_peer(step)
            deal_copy(k, r, dst, dst).start()

        mine = pl.ds(pl.multiple_of(r * CUT, CUT), CUT)
        for p in range(dealt):
            deal[k][r * dealt + p] = pack[k, p, mine, :]
        for s in range(SLOTS):
            got[k][:, cap + s] = own[s].reshape(ROWS, CUT, BS)

    def deal_in(k):
        @pl.loop(1, ROWS)
        def _(step):
            src = row_peer(step)
            deal_copy(k, src, r, src).wait_recv()

    def pick(k, dst, q):
        address = want_s[dst, 0, q]
        row = lax.div(address, BS)
        return deal[k][want_s[row, 0, address - row * BS]]

    def pass_on(k):
        @pl.loop(1, ROWS)
        def _(step):
            dst = row_peer(step)
            for q in range(cap):
                stage[k, dst, q] = pick(k, dst, q)
            got_copy(k, r, dst, dst).start()

        for q in range(cap):
            got[k][r, q] = pick(k, r, q)

    def get_in(k):
        @pl.loop(1, ROWS)
        def _(step):
            src = row_peer(step)
            got_copy(k, src, r, src).wait_recv()

    def right_blocks(k, s):
        places = (cap + s, place_s[2 * s], place_s[2 * s + 1])
        return right_operand([got[k][:, place].reshape(BS, BS) for place in places])

    def by_term(s, values):
        own = first + s
        first_is, second_is, third_is = (right_s[t, 0, s] == own for t in range(3))
        return (
            jnp.where(first_is, values[0], jnp.where(second_is, values[1], values[2])),
            jnp.where(first_is, values[1], values[0]),
            jnp.where(third_is, values[1], values[2]),
        )

    def left_indices(s):
        return by_term(s, [left_s[t, 0, s] for t in range(3)])

    def left_blocks(pan, s):
        blocks = []
        for index in left_indices(s):
            held = jnp.maximum(index, 0)
            owner = lax.div(held, SLOTS)
            near = lax.rem(owner - c + 1 + COLS, COLS)
            place = jnp.minimum(near * SLOTS + held - owner * SLOTS, 3 * SLOTS)
            blocks.append(pan[jnp.where(index >= 0, place, 3 * SLOTS)])
        return left_operand(blocks)

    def mirror_tables():
        table = jnp.zeros((1, BS), jnp.int32)
        to_up, to_down = table, table
        ups, downs = jnp.int32(0), jnp.int32(0)
        for s in range(SLOTS):
            self_left, *others = left_indices(s)
            diagonal = self_left == c * SLOTS + s
            for u, index in enumerate(others):
                e = 2 * s + u
                side = lax.rem(lax.div(jnp.maximum(index, 0), SLOTS) - c + COLS, COLS)
                live = jnp.logical_and(diagonal, index >= 0)
                is_up = jnp.logical_and(live, side == 1)
                is_down = jnp.logical_and(live, side == COLS - 1)
                rank = jnp.minimum(jnp.where(is_up, ups, downs), OFF_DIAG - 1)
                table = jnp.where(lane == e, rank, jnp.where(lane == TARGET + e, index, table))
                to_up = jnp.where(lane == jnp.where(is_up, ups, -1), place_s[e], to_up)
                to_down = jnp.where(lane == jnp.where(is_down, downs, -1), place_s[e], to_down)
                ups, downs = ups + is_up.astype(jnp.int32), downs + is_down.astype(jnp.int32)
        table_v[2] = table
        table_v[3] = to_up
        table_v[4] = to_down

    def mirror(s):
        self_left = left_indices(s)[0]
        owner = lax.div(self_left, SLOTS)
        e = 2 * (self_left - owner * SLOTS)
        side = lax.rem(owner - c + COLS, COLS)
        row = jnp.where(side == COLS - 1, 0, jnp.where(side == 1, 1, 2))
        own = c * SLOTS + s
        e = e + (table_s[row, 0, TARGET + e + 1] == own).astype(jnp.int32)
        place = jnp.where(self_left == own, cap + s, place_s[e])
        near = mirror_in[jnp.where(row == 2, 0, row * OFF_DIAG + table_s[row, 0, e])]
        return jnp.where(row == 2, got_d[:, place].reshape(BS, BS), near)

    @pl.loop(1, ROWS)
    def _(step):
        dst = row_peer(step)
        want_copy(r, dst, dst).start()

    near_d = near_copies(0, own_d, pan_d)
    deal_out(0, own_d)
    for copy in near_d:
        copy.start()

    @pl.loop(1, ROWS)
    def _(step):
        src = row_peer(step)
        want_copy(src, r, src).wait_recv()

    to_smem = pltpu.make_async_copy(want_v, want_s, local_sem.at[5])
    to_smem.start()
    for load in loads[2:]:
        load.wait()
    mirror_tables()
    for copy in table_copies:
        copy.start()
    to_smem.wait()

    deal_in(0)
    pass_on(0)
    deal_out(1, own_h)
    for copy in (*table_copies, *near_d):
        copy.wait_recv()
    tables_to_smem = pltpu.make_async_copy(table_v, table_s, local_sem.at[6])
    tables_to_smem.start()
    tables_to_smem.wait()
    get_in(0)
    for k in range(2):
        for q in range(OFF_DIAG):
            mirror_stage[k, q] = got_d[:, table_s[3 + k, 0, q]].reshape(BS, BS)
        mirror_copies[k].start()

    eye = lax.broadcasted_iota(jnp.int32, (BS, BS), 0) == lax.broadcasted_iota(jnp.int32, (BS, BS), 1)

    def trace_row(block, s):
        on = (left_indices(s)[0] == c * SLOTS + s).astype(jnp.float32)
        return jnp.sum(jnp.where(eye, block, 0.0), axis=0, keepdims=True) * on

    part[...] = jnp.zeros_like(part)

    @pl.loop(0, SLOTS)
    def _(s):
        square = product(left_blocks(pan_d, s), right_blocks(0, s))
        pan_q[SLOTS + s] = square
        own_q[s] = square
        part[0:1, :] += trace_row(own_d[s], s)
        part[1:2, :] += trace_row(square, s)

    near_q = near_copies(1, own_q, pan_q)
    deal_out(2, own_q)
    for copy in near_q:
        copy.start()
    deal_in(1)
    deal_in(2)
    pass_on(2)
    for copy in (*near_q, *mirror_copies):
        copy.wait_recv()

    @pl.loop(0, SLOTS)
    def _(s):
        cube = product(left_blocks(pan_q, s), right_blocks(0, s))
        mix_dir[s] = cube
        part[2:3, :] += trace_row(cube, s)
        part[3:4, :] += jnp.sum(cube.T * mirror(s), axis=0, keepdims=True)

    part[4:5, :] = jnp.zeros((1, BS), jnp.float32) + over

    def row_copy(src, dst, peer):
        return pltpu.make_async_remote_copy(
            src_ref=part, dst_ref=part_row.at[src], send_sem=row_send.at[dst], recv_sem=row_recv.at[src],
            device_id=(peer, c), device_id_type=MESH,
        )

    def col_copy(src, dst, peer):
        return pltpu.make_async_remote_copy(
            src_ref=part_col.at[src], dst_ref=part_col.at[src], send_sem=col_send.at[dst], recv_sem=col_recv.at[src],
            device_id=(r, peer), device_id_type=MESH,
        )

    @pl.loop(1, ROWS)
    def _(step):
        dst = row_peer(step)
        row_copy(r, dst, dst).start()

    part_row[r] = part[...]
    pass_on(1)
    get_in(2)

    @pl.loop(0, SLOTS)
    def _(s):
        fourth = product(left_blocks(pan_q, s), right_blocks(2, s))
        cube = mix_dir[s]
        mix_base[s] = 4.0 * cube - 3.0 * fourth
        mix_dir[s] = fourth - 2.0 * cube + own_q[s]

    @pl.loop(1, ROWS)
    def _(step):
        src = row_peer(step)
        row_copy(src, r, src).wait_recv()

    part_col[c] = jnp.sum(part_row[...], axis=0)

    @pl.loop(1, COLS)
    def _(step):
        dst = col_peer(step)
        col_copy(c, dst, dst).start()

    get_in(1)

    @pl.loop(0, SLOTS)
    def _(s):
        ew_v[s] = product(left_blocks(pan_q, s), right_blocks(1, s))

    put_ew = pltpu.make_async_copy(ew_v, ew_ref, local_sem.at[7])
    put_ew.start()

    @pl.loop(1, COLS)
    def _(step):
        src = col_peer(step)
        col_copy(src, c, src).wait_recv()

    sums = jnp.sum(part_col[...], axis=0)
    over_ref[0, 0] = jnp.sum(sums[4:5, :])
    traces = jnp.sum(sums, axis=1, keepdims=True)
    one, two, three, four = (traces[k : k + 1, :] for k in range(4))
    trace_f = 4.0 * three - 3.0 * four
    trace_g = four - 2.0 * three + two
    gamma = jnp.clip((one - trace_f) / jnp.maximum(jnp.abs(trace_g), 1.0), 0.0, 6.0)

    @pl.loop(0, SLOTS)
    def _(s):
        new_v[s] = mix_base[s] + gamma * mix_dir[s]

    put_new = pltpu.make_async_copy(new_v, new_ref, local_sem.at[8])
    put_new.start()

    for copy in (*near_d, *near_q, *table_copies, *mirror_copies):
        copy.wait_send()

    @pl.loop(1, ROWS)
    def _(step):
        dst = row_peer(step)
        want_copy(r, dst, dst).wait_send()
        row_copy(r, dst, dst).wait_send()
        for k in range(3):
            deal_copy(k, r, dst, dst).wait_send()
            got_copy(k, r, dst, dst).wait_send()

    @pl.loop(1, COLS)
    def _(step):
        dst = col_peer(step)
        col_copy(c, dst, dst).wait_send()

    put_ew.wait()
    put_new.wait()


def step(cap, dealt, collective_id, *operands):
    any_space = pl.BlockSpec(memory_space=pl.ANY)
    smem = pl.BlockSpec(memory_space=pltpu.SMEM)
    block = jax.ShapeDtypeStruct((SLOTS, BS, BS), jnp.float32)
    dma = pltpu.SemaphoreType.DMA
    panel = pltpu.VMEM((3 * SLOTS + 1, BS, BS), jnp.float32)
    own = pltpu.VMEM((SLOTS, BS, BS), jnp.float32)
    slices = pltpu.VMEM((ROWS * dealt, CUT, BS), jnp.float32)
    fetched = pltpu.VMEM((ROWS, cap + SLOTS, CUT, BS), jnp.float32)
    return pl.pallas_call(
        functools.partial(kernel, cap, dealt),
        out_shape=(block, block, jax.ShapeDtypeStruct((1, 1), jnp.float32)),
        in_specs=[any_space] * 4,
        out_specs=(any_space, any_space, smem),
        scratch_shapes=[
            panel,
            panel,
            own,
            own,
            own,
            pltpu.VMEM((3, dealt, BS, BS), jnp.float32),
            slices,
            slices,
            slices,
            pltpu.VMEM((3, ROWS, cap, CUT, BS), jnp.float32),
            fetched,
            fetched,
            fetched,
            own,
            own,
            own,
            own,
            pltpu.VMEM((2, OFF_DIAG, BS, BS), jnp.float32),
            pltpu.VMEM((2 * OFF_DIAG, BS, BS), jnp.float32),
            pltpu.SMEM((3, 1, SLOTS), jnp.int32),
            pltpu.SMEM((3, 1, SLOTS), jnp.int32),
            pltpu.SMEM((WANT_MOST,), jnp.int32),
            pltpu.VMEM((5, 1, BS), jnp.int32),
            pltpu.SMEM((5, 1, BS), jnp.int32),
            pltpu.VMEM((ROWS, 1, BS), jnp.int32),
            pltpu.SMEM((ROWS, 1, BS), jnp.int32),
            pltpu.VMEM((8, BS), jnp.float32),
            pltpu.VMEM((ROWS, 8, BS), jnp.float32),
            pltpu.VMEM((COLS, 8, BS), jnp.float32),
            dma((9,)),
            dma((2, 2)),
            dma((2, 2)),
            dma((3, ROWS)),
            dma((3, ROWS)),
            dma((3, ROWS)),
            dma((3, ROWS)),
            dma((ROWS,)),
            dma((ROWS,)),
            dma((ROWS,)),
            dma((ROWS,)),
            dma((COLS,)),
            dma((COLS,)),
            dma((2,)),
            dma((2,)),
            dma((2,)),
            dma((2,)),
        ],
        compiler_params=pltpu.CompilerParams(
            collective_id=collective_id, has_side_effects=True, vmem_limit_bytes=60 * 1024 * 1024
        ),
        cost_estimate=pl.CostEstimate(flops=2 * 9 * 4 * SLOTS * BS**3, bytes_accessed=5 * SLOTS * BS * BS, transcendentals=0),
    )(*operands)


def shards(density, hamiltonian, block_rows, block_cols, left_index, right_index):
    terms_first = (2, 0, 1)
    operands = (
        density[0], hamiltonian[0],
        jnp.transpose(left_index, terms_first), jnp.transpose(right_index, terms_first),
    )
    new, ew, over = step(WANT_FEW, min(WANT_FEW, SLOTS), 0, *operands)
    new, ew = lax.cond(
        over[0, 0] > 0.0,
        lambda new, ew, *operands: tuple(step(WANT_MOST, SLOTS, 1, *operands)[:2]),
        lambda new, ew, *operands: (new, ew),
        new, ew, *operands,
    )
    return new[None], ew[None]


def solution(mesh):
    in_specs = (
        P("row", "col", None, None),
        P("row", "col", None, None),
        P("row", "col"),
        P("row", "col"),
        P("row", "col", None),
        P("row", "col", None),
    )
    out_specs = (P("row", "col", None, None), P("row", "col", None, None))
    return jax.shard_map(shards, mesh=mesh, in_specs=in_specs, out_specs=out_specs, check_vma=False)
```

```python
import functools

import jax
import jax.numpy as jnp
from jax import lax
from jax.experimental import pallas as pl
from jax.experimental.pallas import tpu as pltpu
from jax.sharding import PartitionSpec as P

MESH = pl.DeviceIdType.MESH
ROWS = 16
COLS = 8
SLOTS = 10
BS = 128
CUT = BS // ROWS
OTHERS = 2
WANT_MOST = SLOTS * OTHERS
WANT_FEW = 8
OFF_DIAG = 6
TARGET = 32
UNROLL = 10
EARLY = 1
PLACES = 64


def halves(x):
    high = x.astype(jnp.bfloat16)
    low = (x - high.astype(jnp.float32)).astype(jnp.bfloat16)
    return high, low


def left_operand(blocks):
    pairs = [halves(block) for block in blocks]
    parts = [half for pair in pairs for half in pair] + [high for high, _ in pairs]
    return jnp.concatenate(parts, axis=1)


def right_operand(blocks):
    pairs = [halves(block) for block in blocks]
    parts = [high for high, _ in pairs for _ in range(2)] + [low for _, low in pairs]
    return jnp.concatenate(parts, axis=0)


def product(left, right):
    return jnp.dot(left, right, preferred_element_type=jnp.float32)


def kernel(
    cap, dealt, quick,
    d_ref, h_ref, left_ref, right_ref,
    new_ref, ew_ref, over_ref,
    pan_d, pan_q, own_d, own_h, own_q, pack, deal_d, deal_h, deal_q, stage, got_d, got_h, got_q, cube_v, turned_v, new_v, ew_v,
    mirror_stage, mirror_in, left_s, right_s, place_s, table_v, table_s, want_v, want_s, part, part_row, part_col,
    local_sem, put_sem, near_send, near_recv, deal_send, deal_recv, got_send, got_recv,
    want_send, want_recv, row_send, row_recv, col_send, col_recv, table_send, table_recv, mirror_send, mirror_recv,
):
    r, c = lax.axis_index("row"), lax.axis_index("col")
    up, down = lax.rem(c + 1, COLS), lax.rem(c + COLS - 1, COLS)
    first = r * SLOTS
    deal, got = (deal_d, deal_h, deal_q), (got_d, got_h, got_q)
    middle = pl.ds(SLOTS, SLOTS)

    def row_peer(step):
        return lax.rem(r + step, ROWS)

    def col_peer(step):
        return lax.rem(c + step, COLS)

    loads = [
        pltpu.make_async_copy(src, dst, local_sem.at[k])
        for k, (src, dst) in enumerate(
            (
                (right_ref, right_s),
                (d_ref, own_d),
                (d_ref, pan_d.at[middle]),
                (left_ref, left_s),
                (h_ref, own_h),
            )
        )
    ]
    for load in loads:
        load.start()

    barrier = pltpu.get_barrier_semaphore()

    @pl.loop(1, ROWS)
    def _(step):
        pl.semaphore_signal(barrier, inc=1, device_id=(row_peer(step), c), device_id_type=MESH)

    @pl.loop(1, COLS)
    def _(step):
        pl.semaphore_signal(barrier, inc=1, device_id=(r, col_peer(step)), device_id_type=MESH)

    loads[0].wait()

    lane = lax.broadcasted_iota(jnp.int32, (1, BS), 1)
    wanted = jnp.full((1, BS), PLACES, jnp.int32)
    count, packed = jnp.int32(0), jnp.int32(0)
    slots = [jnp.int32(p) for p in range(dealt)]
    for s in range(SLOTS):
        own = first + s
        one, two, three = (right_s[t, 0, s] for t in range(3))
        lone = True
        for u, index in enumerate((jnp.where(one == own, two, one), jnp.where(three == own, two, three))):
            live = index >= 0
            near = index - first
            here = jnp.logical_and(near >= 0, near < SLOTS)
            away = jnp.logical_and(live, jnp.logical_not(here))
            lone = jnp.logical_and(lone, jnp.logical_not(away))
            place_s[2 * s + u] = jnp.where(away, jnp.minimum(count, cap - 1), jnp.where(here, cap + near, 0))
            held = jnp.maximum(index, 0)
            owner = lax.div(held, SLOTS)
            address = owner * BS + PLACES + held - owner * SLOTS
            wanted = jnp.where(lane == jnp.where(away, count, -1), address, wanted)
            count = count + away.astype(jnp.int32)
        if dealt == SLOTS:
            wanted = jnp.where(lane == PLACES + s, r * dealt + s, wanted)
        else:
            wanted = jnp.where(lane == PLACES + s, r * dealt + jnp.minimum(packed, dealt - 1), wanted)
            here = jnp.where(lone, -1, packed)
            for p in range(min(s + 1, dealt)):
                slots[p] = jnp.where(here == p, s, slots[p])
            packed = packed + jnp.logical_not(lone).astype(jnp.int32)
    want_v[r] = wanted

    zero_block = jnp.zeros((BS, BS), jnp.float32)
    pan_d[3 * SLOTS] = zero_block
    pan_q[3 * SLOTS] = zero_block
    loads[1].wait()

    pl.semaphore_wait(barrier, ROWS + COLS - 2)

    def want_copy(src, dst, peer):
        return pltpu.make_async_remote_copy(
            src_ref=want_v.at[src], dst_ref=want_v.at[src], send_sem=want_send.at[dst], recv_sem=want_recv.at[src],
            device_id=(peer, c), device_id_type=MESH,
        )

    def deal_copy(k, src, dst, peer):
        return pltpu.make_async_remote_copy(
            src_ref=pack.at[k, :, pl.ds(pl.multiple_of(dst * CUT, CUT), CUT), :],
            dst_ref=deal[k].at[pl.ds(src * dealt, dealt)],
            send_sem=deal_send.at[k, dst], recv_sem=deal_recv.at[k, src],
            device_id=(peer, c), device_id_type=MESH,
        )

    def got_copy(k, src, dst, peer):
        return pltpu.make_async_remote_copy(
            src_ref=stage.at[k, dst], dst_ref=got[k].at[src, pl.ds(0, cap)],
            send_sem=got_send.at[k, dst], recv_sem=got_recv.at[k, src],
            device_id=(peer, c), device_id_type=MESH,
        )

    def near_copies(k, own, pan):
        to_up = pltpu.make_async_remote_copy(
            src_ref=own, dst_ref=pan.at[pl.ds(0, SLOTS)],
            send_sem=near_send.at[k, 0], recv_sem=near_recv.at[k, 0],
            device_id=(r, up), device_id_type=MESH,
        )
        to_down = pltpu.make_async_remote_copy(
            src_ref=own, dst_ref=pan.at[pl.ds(2 * SLOTS, SLOTS)],
            send_sem=near_send.at[k, 1], recv_sem=near_recv.at[k, 1],
            device_id=(r, down), device_id_type=MESH,
        )
        return to_up, to_down

    table_copies = [
        pltpu.make_async_remote_copy(
            src_ref=table_v.at[2], dst_ref=table_v.at[k], send_sem=table_send.at[k], recv_sem=table_recv.at[k],
            device_id=(r, peer), device_id_type=MESH,
        )
        for k, peer in enumerate((up, down))
    ]
    mirror_copies = [
        pltpu.make_async_remote_copy(
            src_ref=mirror_stage.at[k], dst_ref=mirror_in.at[pl.ds(k * OFF_DIAG, OFF_DIAG)],
            send_sem=mirror_send.at[k], recv_sem=mirror_recv.at[k],
            device_id=(r, peer), device_id_type=MESH,
        )
        for k, peer in enumerate((up, down))
    ]

    def deal_out(k, own):
        for p in range(dealt):
            pack[k, p] = own[slots[p]]

        @pl.loop(1, ROWS)
        def _(step):
            dst = row_peer(step)
            deal_copy(k, r, dst, dst).start()

        mine = pl.ds(pl.multiple_of(r * CUT, CUT), CUT)
        for p in range(dealt):
            deal[k][r * dealt + p] = pack[k, p, mine, :]
        for s in range(SLOTS):
            got[k][:, cap + s] = own[s].reshape(ROWS, CUT, BS)

    def deal_in(k):
        @pl.loop(1, ROWS)
        def _(step):
            src = row_peer(step)
            deal_copy(k, src, r, src).wait_recv()

    def pick(k, dst, q):
        address = want_s[dst, 0, q]
        row = lax.div(address, BS)
        return deal[k][want_s[row, 0, address - row * BS]]

    def pass_on(k, low, high):
        @pl.loop(low, high)
        def _(step):
            dst = row_peer(step)
            for q in range(cap):
                stage[k, dst, q] = pick(k, dst, q)
            got_copy(k, r, dst, dst).start()

        if high == ROWS:
            for q in range(cap):
                got[k][r, q] = pick(k, r, q)

    def get_in(k):
        @pl.loop(1, ROWS)
        def _(step):
            src = row_peer(step)
            got_copy(k, src, r, src).wait_recv()

    def right_blocks(k, s):
        places = (cap + s, place_s[2 * s], place_s[2 * s + 1])
        return right_operand([got[k][:, place].reshape(BS, BS) for place in places])

    def by_term(s, values):
        own = first + s
        first_is, second_is, third_is = (right_s[t, 0, s] == own for t in range(3))
        return (
            jnp.where(first_is, values[0], jnp.where(second_is, values[1], values[2])),
            jnp.where(first_is, values[1], values[0]),
            jnp.where(third_is, values[1], values[2]),
        )

    def left_indices(s):
        return by_term(s, [left_s[t, 0, s] for t in range(3)])

    def panel_block(pan, index):
        held = jnp.maximum(index, 0)
        owner = lax.div(held, SLOTS)
        near = lax.rem(owner - c + 1 + COLS, COLS)
        place = jnp.minimum(near * SLOTS + held - owner * SLOTS, 3 * SLOTS)
        return pan[jnp.where(index >= 0, place, 3 * SLOTS)]

    def left_blocks(pan, s):
        return left_operand([panel_block(pan, index) for index in left_indices(s)])

    def mirror_tables():
        threes = jnp.int32(0)
        table = jnp.zeros((1, BS), jnp.int32)
        to_up, to_down = table, table
        ups, downs = jnp.int32(0), jnp.int32(0)
        for s in range(SLOTS):
            self_left, *others = left_indices(s)
            diagonal = self_left == c * SLOTS + s
            three = jnp.logical_and(jnp.logical_not(diagonal), others[1] >= 0)
            threes = threes + three.astype(jnp.int32)
            for u, index in enumerate(others):
                e = 2 * s + u
                side = lax.rem(lax.div(jnp.maximum(index, 0), SLOTS) - c + COLS, COLS)
                live = jnp.logical_and(diagonal, index >= 0)
                is_up = jnp.logical_and(live, side == 1)
                is_down = jnp.logical_and(live, side == COLS - 1)
                rank = jnp.minimum(jnp.where(is_up, ups, downs), OFF_DIAG - 1)
                table = jnp.where(lane == e, rank, jnp.where(lane == TARGET + e, index, table))
                to_up = jnp.where(lane == jnp.where(is_up, ups, -1), place_s[e], to_up)
                to_down = jnp.where(lane == jnp.where(is_down, downs, -1), place_s[e], to_down)
                ups, downs = ups + is_up.astype(jnp.int32), downs + is_down.astype(jnp.int32)
        table_v[2] = table
        table_v[3] = to_up
        table_v[4] = to_down
        return threes

    def mirror(s):
        self_left = left_indices(s)[0]
        owner = lax.div(self_left, SLOTS)
        e = 2 * (self_left - owner * SLOTS)
        side = lax.rem(owner - c + COLS, COLS)
        row = jnp.where(side == COLS - 1, 0, jnp.where(side == 1, 1, 2))
        own = c * SLOTS + s
        e = e + (table_s[row, 0, TARGET + e + 1] == own).astype(jnp.int32)
        place = jnp.where(self_left == own, cap + s, place_s[e])
        near = mirror_in[jnp.where(row == 2, 0, row * OFF_DIAG + table_s[row, 0, e])]
        return jnp.where(row == 2, got_d[:, place].reshape(BS, BS), near)

    @pl.loop(1, ROWS)
    def _(step):
        dst = row_peer(step)
        want_copy(r, dst, dst).start()

    near_d = near_copies(0, own_d, pan_d)
    deal_out(0, own_d)
    for copy in near_d:
        copy.start()

    @pl.loop(1, ROWS)
    def _(step):
        src = row_peer(step)
        want_copy(src, r, src).wait_recv()

    to_smem = pltpu.make_async_copy(want_v, want_s, local_sem.at[5])
    to_smem.start()
    for load in loads[2:]:
        load.wait()
    threes = mirror_tables()
    over = jnp.where(jnp.logical_or(count > cap, threes > 0), 1.0, 0.0)
    for copy in table_copies:
        copy.start()
    to_smem.wait()

    deal_in(0)
    pass_on(0, 1, ROWS)
    deal_out(1, own_h)
    for copy in (*table_copies, *near_d):
        copy.wait_recv()
    tables_to_smem = pltpu.make_async_copy(table_v, table_s, local_sem.at[6])
    tables_to_smem.start()
    tables_to_smem.wait()
    get_in(0)
    for k in range(2):
        for q in range(OFF_DIAG):
            mirror_stage[k, q] = got_d[:, table_s[3 + k, 0, q]].reshape(BS, BS)
        mirror_copies[k].start()

    eye = lax.broadcasted_iota(jnp.int32, (BS, BS), 0) == lax.broadcasted_iota(jnp.int32, (BS, BS), 1)

    def trace_row(block, s):
        on = (left_indices(s)[0] == c * SLOTS + s).astype(jnp.float32)
        return jnp.sum(jnp.where(eye, block, 0.0), axis=0, keepdims=True) * on

    part[...] = jnp.zeros_like(part)

    @pl.loop(0, SLOTS, unroll=UNROLL)
    def _(s):
        square = product(left_blocks(pan_d, s), right_blocks(0, s))
        pan_q[SLOTS + s] = square
        own_q[s] = square
        part[0:1, :] += trace_row(own_d[s], s)
        part[1:2, :] += trace_row(square, s)

    def row_copy(src, dst, peer):
        return pltpu.make_async_remote_copy(
            src_ref=part, dst_ref=part_row.at[src], send_sem=row_send.at[dst], recv_sem=row_recv.at[src],
            device_id=(peer, c), device_id_type=MESH,
        )

    def col_copy(src, dst, peer):
        return pltpu.make_async_remote_copy(
            src_ref=part_col.at[src], dst_ref=part_col.at[src], send_sem=col_send.at[dst], recv_sem=col_recv.at[src],
            device_id=(r, peer), device_id_type=MESH,
        )

    def sum_rows_start():
        part[4:5, :] = jnp.zeros((1, BS), jnp.float32) + over

        @pl.loop(1, ROWS)
        def _(step):
            dst = row_peer(step)
            row_copy(r, dst, dst).start()

        part_row[r] = part[...]

    def sum_cols_start():
        @pl.loop(1, ROWS)
        def _(step):
            src = row_peer(step)
            row_copy(src, r, src).wait_recv()

        part_col[c] = jnp.sum(part_row[...], axis=0)

        @pl.loop(1, COLS)
        def _(step):
            dst = col_peer(step)
            col_copy(c, dst, dst).start()

    def trace_factors():
        @pl.loop(0, SLOTS, unroll=UNROLL)
        def _(s):
            square = own_q[s]
            turned = square.T
            self_left = left_indices(s)[0]
            corner = got_d[:, place_s[2 * s]].reshape(BS, BS)
            left = left_operand([square, panel_block(pan_d, self_left)])
            factor = product(left, right_operand([corner, square]))
            on = self_left == c * SLOTS + s
            turned_v[0, s] = turned
            turned_v[1, s] = jnp.where(on, 0.0, factor.T)
            part[3:4, :] += jnp.sum(jnp.where(on, turned * square, 0.0), axis=0, keepdims=True)

    def traces_without_triangles():
        @pl.loop(0, SLOTS, unroll=UNROLL)
        def _(s):
            back = mirror(s)
            part[2:3, :] += jnp.sum(turned_v[0, s] * back, axis=0, keepdims=True)
            part[3:4, :] += jnp.sum(turned_v[1, s] * back, axis=0, keepdims=True)

    def find_gamma():
        @pl.loop(1, COLS)
        def _(step):
            src = col_peer(step)
            col_copy(src, c, src).wait_recv()

        sums = jnp.sum(part_col[...], axis=0)
        over_ref[0, 0] = jnp.sum(sums[4:5, :])
        traces = jnp.sum(sums, axis=1, keepdims=True)
        one, two, three, four = (traces[k : k + 1, :] for k in range(4))
        trace_f = 4.0 * three - 3.0 * four
        trace_g = four - 2.0 * three + two
        return jnp.clip((one - trace_f) / jnp.maximum(jnp.abs(trace_g), 1.0), 0.0, 6.0)

    def put(k, src, dst, s):
        return pltpu.make_async_copy(src.at[s], dst.at[s], put_sem.at[k, s])

    def make_cube():
        @pl.loop(0, SLOTS, unroll=UNROLL)
        def _(s):
            cube = product(left_blocks(pan_q, s), right_blocks(0, s))
            cube_v[s] = cube
            if not quick:
                part[2:3, :] += trace_row(cube, s)
                part[3:4, :] += jnp.sum(cube.T * mirror(s), axis=0, keepdims=True)

    def make_new(gamma):
        @pl.loop(0, SLOTS, unroll=UNROLL)
        def _(s):
            fourth = product(left_blocks(pan_q, s), right_blocks(2, s))
            cube = cube_v[s]
            new_v[s] = 4.0 * cube - 3.0 * fourth + gamma * (fourth - 2.0 * cube + own_q[s])
            put(0, new_v, new_ref, s).start()

    def make_energy():
        @pl.loop(0, SLOTS, unroll=UNROLL)
        def _(s):
            ew_v[s] = product(left_blocks(pan_q, s), right_blocks(1, s))
            put(1, ew_v, ew_ref, s).start()

    near_q = near_copies(1, own_q, pan_q)
    deal_out(2, own_q)
    for copy in near_q:
        copy.start()
    if quick:
        trace_factors()
        for copy in mirror_copies:
            copy.wait_recv()
        traces_without_triangles()
        sum_rows_start()
    deal_in(1)
    pass_on(1, 1, EARLY)
    deal_in(2)
    pass_on(2, 1, ROWS)
    pass_on(1, EARLY, ROWS)
    if quick:
        sum_cols_start()
    else:
        for copy in mirror_copies:
            copy.wait_recv()
    for copy in near_q:
        copy.wait_recv()
    make_cube()
    if not quick:
        sum_rows_start()
        sum_cols_start()
    gamma = find_gamma()
    if EARLY == ROWS:
        get_in(1)
        make_energy()
        get_in(2)
        make_new(gamma)
    else:
        get_in(2)
        make_new(gamma)
        get_in(1)
        make_energy()

    for copy in (*near_d, *near_q, *table_copies, *mirror_copies):
        copy.wait_send()

    @pl.loop(1, ROWS)
    def _(step):
        dst = row_peer(step)
        want_copy(r, dst, dst).wait_send()
        row_copy(r, dst, dst).wait_send()
        for k in range(3):
            deal_copy(k, r, dst, dst).wait_send()
            got_copy(k, r, dst, dst).wait_send()

    @pl.loop(1, COLS)
    def _(step):
        dst = col_peer(step)
        col_copy(c, dst, dst).wait_send()

    @pl.loop(0, SLOTS)
    def _(s):
        put(0, new_v, new_ref, s).wait()
        put(1, ew_v, ew_ref, s).wait()


def step(cap, dealt, quick, collective_id, *operands):
    any_space = pl.BlockSpec(memory_space=pl.ANY)
    smem = pl.BlockSpec(memory_space=pltpu.SMEM)
    block = jax.ShapeDtypeStruct((SLOTS, BS, BS), jnp.float32)
    dma = pltpu.SemaphoreType.DMA
    panel = pltpu.VMEM((3 * SLOTS + 1, BS, BS), jnp.float32)
    own = pltpu.VMEM((SLOTS, BS, BS), jnp.float32)
    slices = pltpu.VMEM((ROWS * dealt, CUT, BS), jnp.float32)
    fetched = pltpu.VMEM((ROWS, cap + SLOTS, CUT, BS), jnp.float32)
    return pl.pallas_call(
        functools.partial(kernel, cap, dealt, quick),
        out_shape=(block, block, jax.ShapeDtypeStruct((1, 1), jnp.float32)),
        in_specs=[any_space] * 4,
        out_specs=(any_space, any_space, smem),
        scratch_shapes=[
            panel,
            panel,
            own,
            own,
            own,
            pltpu.VMEM((3, dealt, BS, BS), jnp.float32),
            slices,
            slices,
            slices,
            pltpu.VMEM((3, ROWS, cap, CUT, BS), jnp.float32),
            fetched,
            fetched,
            fetched,
            own,
            pltpu.VMEM((2, SLOTS, BS, BS), jnp.float32),
            own,
            own,
            pltpu.VMEM((2, OFF_DIAG, BS, BS), jnp.float32),
            pltpu.VMEM((2 * OFF_DIAG, BS, BS), jnp.float32),
            pltpu.SMEM((3, 1, SLOTS), jnp.int32),
            pltpu.SMEM((3, 1, SLOTS), jnp.int32),
            pltpu.SMEM((WANT_MOST,), jnp.int32),
            pltpu.VMEM((5, 1, BS), jnp.int32),
            pltpu.SMEM((5, 1, BS), jnp.int32),
            pltpu.VMEM((ROWS, 1, BS), jnp.int32),
            pltpu.SMEM((ROWS, 1, BS), jnp.int32),
            pltpu.VMEM((8, BS), jnp.float32),
            pltpu.VMEM((ROWS, 8, BS), jnp.float32),
            pltpu.VMEM((COLS, 8, BS), jnp.float32),
            dma((9,)),
            dma((2, SLOTS)),
            dma((2, 2)),
            dma((2, 2)),
            dma((3, ROWS)),
            dma((3, ROWS)),
            dma((3, ROWS)),
            dma((3, ROWS)),
            dma((ROWS,)),
            dma((ROWS,)),
            dma((ROWS,)),
            dma((ROWS,)),
            dma((COLS,)),
            dma((COLS,)),
            dma((2,)),
            dma((2,)),
            dma((2,)),
            dma((2,)),
        ],
        compiler_params=pltpu.CompilerParams(
            collective_id=collective_id, has_side_effects=True, vmem_limit_bytes=60 * 1024 * 1024
        ),
        cost_estimate=pl.CostEstimate(flops=2 * 9 * 4 * SLOTS * BS**3, bytes_accessed=5 * SLOTS * BS * BS, transcendentals=0),
    )(*operands)


def shards(density, hamiltonian, block_rows, block_cols, left_index, right_index):
    terms_first = (2, 0, 1)
    operands = (
        density[0], hamiltonian[0],
        jnp.transpose(left_index, terms_first), jnp.transpose(right_index, terms_first),
    )
    new, ew, over = step(WANT_FEW, min(WANT_FEW, SLOTS), True, 0, *operands)
    new, ew = lax.cond(
        over[0, 0] > 0.0,
        lambda new, ew, *operands: tuple(step(WANT_MOST, SLOTS, False, 1, *operands)[:2]),
        lambda new, ew, *operands: (new, ew),
        new, ew, *operands,
    )
    return new[None], ew[None]


def solution(mesh):
    in_specs = (
        P("row", "col", None, None),
        P("row", "col", None, None),
        P("row", "col"),
        P("row", "col"),
        P("row", "col", None),
        P("row", "col", None),
    )
    out_specs = (P("row", "col", None, None), P("row", "col", None, None))
    return jax.shard_map(shards, mesh=mesh, in_specs=in_specs, out_specs=out_specs, check_vma=False)
```

```python
import functools

import jax
import jax.numpy as jnp
from jax import lax
from jax.experimental import pallas as pl
from jax.experimental.pallas import tpu as pltpu
from jax.sharding import PartitionSpec as P

MESH = pl.DeviceIdType.MESH
ROWS = 16
COLS = 8
SLOTS = 10
BS = 128
CUT = BS // ROWS
OTHERS = 2
WANT_MOST = SLOTS * OTHERS
WANT_FEW = 8
OFF_DIAG = 6
TARGET = 32
UNROLL = 10
EARLY = ROWS
PLACES = 64


def halves(x):
    high = x.astype(jnp.bfloat16)
    low = (x - high.astype(jnp.float32)).astype(jnp.bfloat16)
    return high, low


def left_operand(blocks):
    pairs = [halves(block) for block in blocks]
    parts = [half for pair in pairs for half in pair] + [high for high, _ in pairs]
    return jnp.concatenate(parts, axis=1)


def right_operand(blocks):
    pairs = [halves(block) for block in blocks]
    parts = [high for high, _ in pairs for _ in range(2)] + [low for _, low in pairs]
    return jnp.concatenate(parts, axis=0)


def product(left, right):
    return jnp.dot(left, right, preferred_element_type=jnp.float32)


def kernel(
    cap, dealt, quick,
    d_ref, h_ref, left_ref, right_ref,
    new_ref, ew_ref, over_ref,
    pan_d, pan_q, own_d, own_h, own_q, pack, deal_d, deal_h, deal_q, stage, got_d, got_h, got_q, cube_v, turned_v,
    mirror_stage, mirror_in, left_s, right_s, place_s, table_v, table_s, want_v, want_s, part, part_row, part_col,
    local_sem, near_send, near_recv, deal_send, deal_recv, got_send, got_recv,
    want_send, want_recv, row_send, row_recv, col_send, col_recv, table_send, table_recv, mirror_send, mirror_recv,
):
    r, c = lax.axis_index("row"), lax.axis_index("col")
    up, down = lax.rem(c + 1, COLS), lax.rem(c + COLS - 1, COLS)
    first = r * SLOTS
    deal, got = (deal_d, deal_h, deal_q), (got_d, got_h, got_q)
    middle = pl.ds(SLOTS, SLOTS)

    def row_peer(step):
        return lax.rem(r + step, ROWS)

    def col_peer(step):
        return lax.rem(c + step, COLS)

    loads = [
        pltpu.make_async_copy(src, dst, local_sem.at[k])
        for k, (src, dst) in enumerate(
            (
                (right_ref, right_s),
                (d_ref, own_d),
                (d_ref, pan_d.at[middle]),
                (left_ref, left_s),
                (h_ref, own_h),
            )
        )
    ]
    for load in loads:
        load.start()

    barrier = pltpu.get_barrier_semaphore()

    @pl.loop(1, ROWS)
    def _(step):
        pl.semaphore_signal(barrier, inc=1, device_id=(row_peer(step), c), device_id_type=MESH)

    @pl.loop(1, COLS)
    def _(step):
        pl.semaphore_signal(barrier, inc=1, device_id=(r, col_peer(step)), device_id_type=MESH)

    loads[0].wait()

    lane = lax.broadcasted_iota(jnp.int32, (1, BS), 1)
    wanted = jnp.full((1, BS), PLACES, jnp.int32)
    count, packed = jnp.int32(0), jnp.int32(0)
    slots = [jnp.int32(p) for p in range(dealt)]
    for s in range(SLOTS):
        own = first + s
        one, two, three = (right_s[t, 0, s] for t in range(3))
        lone = True
        for u, index in enumerate((jnp.where(one == own, two, one), jnp.where(three == own, two, three))):
            live = index >= 0
            near = index - first
            here = jnp.logical_and(near >= 0, near < SLOTS)
            away = jnp.logical_and(live, jnp.logical_not(here))
            lone = jnp.logical_and(lone, jnp.logical_not(away))
            place_s[2 * s + u] = jnp.where(away, jnp.minimum(count, cap - 1), jnp.where(here, cap + near, 0))
            held = jnp.maximum(index, 0)
            owner = lax.div(held, SLOTS)
            address = owner * BS + PLACES + held - owner * SLOTS
            wanted = jnp.where(lane == jnp.where(away, count, -1), address, wanted)
            count = count + away.astype(jnp.int32)
        if dealt == SLOTS:
            wanted = jnp.where(lane == PLACES + s, r * dealt + s, wanted)
        else:
            wanted = jnp.where(lane == PLACES + s, r * dealt + jnp.minimum(packed, dealt - 1), wanted)
            here = jnp.where(lone, -1, packed)
            for p in range(min(s + 1, dealt)):
                slots[p] = jnp.where(here == p, s, slots[p])
            packed = packed + jnp.logical_not(lone).astype(jnp.int32)
    want_v[r] = wanted

    zero_block = jnp.zeros((BS, BS), jnp.float32)
    pan_d[3 * SLOTS] = zero_block
    pan_q[3 * SLOTS] = zero_block
    loads[1].wait()

    pl.semaphore_wait(barrier, ROWS + COLS - 2)

    def want_copy(src, dst, peer):
        return pltpu.make_async_remote_copy(
            src_ref=want_v.at[src], dst_ref=want_v.at[src], send_sem=want_send.at[dst], recv_sem=want_recv.at[src],
            device_id=(peer, c), device_id_type=MESH,
        )

    def deal_copy(k, src, dst, peer):
        return pltpu.make_async_remote_copy(
            src_ref=pack.at[k, :, pl.ds(pl.multiple_of(dst * CUT, CUT), CUT), :],
            dst_ref=deal[k].at[pl.ds(src * dealt, dealt)],
            send_sem=deal_send.at[k, dst], recv_sem=deal_recv.at[k, src],
            device_id=(peer, c), device_id_type=MESH,
        )

    def got_copy(k, src, dst, peer):
        return pltpu.make_async_remote_copy(
            src_ref=stage.at[k, dst], dst_ref=got[k].at[src, pl.ds(0, cap)],
            send_sem=got_send.at[k, dst], recv_sem=got_recv.at[k, src],
            device_id=(peer, c), device_id_type=MESH,
        )

    def near_copies(k, own, pan):
        to_up = pltpu.make_async_remote_copy(
            src_ref=own, dst_ref=pan.at[pl.ds(0, SLOTS)],
            send_sem=near_send.at[k, 0], recv_sem=near_recv.at[k, 0],
            device_id=(r, up), device_id_type=MESH,
        )
        to_down = pltpu.make_async_remote_copy(
            src_ref=own, dst_ref=pan.at[pl.ds(2 * SLOTS, SLOTS)],
            send_sem=near_send.at[k, 1], recv_sem=near_recv.at[k, 1],
            device_id=(r, down), device_id_type=MESH,
        )
        return to_up, to_down

    table_copies = [
        pltpu.make_async_remote_copy(
            src_ref=table_v.at[2], dst_ref=table_v.at[k], send_sem=table_send.at[k], recv_sem=table_recv.at[k],
            device_id=(r, peer), device_id_type=MESH,
        )
        for k, peer in enumerate((up, down))
    ]
    mirror_copies = [
        pltpu.make_async_remote_copy(
            src_ref=mirror_stage.at[k], dst_ref=mirror_in.at[pl.ds(k * OFF_DIAG, OFF_DIAG)],
            send_sem=mirror_send.at[k], recv_sem=mirror_recv.at[k],
            device_id=(r, peer), device_id_type=MESH,
        )
        for k, peer in enumerate((up, down))
    ]

    def deal_out(k, own):
        for p in range(dealt):
            pack[k, p] = own[slots[p]]

        @pl.loop(1, ROWS)
        def _(step):
            dst = row_peer(step)
            deal_copy(k, r, dst, dst).start()

        mine = pl.ds(pl.multiple_of(r * CUT, CUT), CUT)
        for p in range(dealt):
            deal[k][r * dealt + p] = pack[k, p, mine, :]
        for s in range(SLOTS):
            got[k][:, cap + s] = own[s].reshape(ROWS, CUT, BS)

    def deal_in(k):
        @pl.loop(1, ROWS)
        def _(step):
            src = row_peer(step)
            deal_copy(k, src, r, src).wait_recv()

    def pick(k, dst, q):
        address = want_s[dst, 0, q]
        row = lax.div(address, BS)
        return deal[k][want_s[row, 0, address - row * BS]]

    def pass_on(k, low, high):
        @pl.loop(low, high)
        def _(step):
            dst = row_peer(step)
            for q in range(cap):
                stage[k, dst, q] = pick(k, dst, q)
            got_copy(k, r, dst, dst).start()

        if high == ROWS:
            for q in range(cap):
                got[k][r, q] = pick(k, r, q)

    def get_in(k):
        @pl.loop(1, ROWS)
        def _(step):
            src = row_peer(step)
            got_copy(k, src, r, src).wait_recv()

    def right_blocks(k, s):
        places = (cap + s, place_s[2 * s], place_s[2 * s + 1])
        return right_operand([got[k][:, place].reshape(BS, BS) for place in places])

    def by_term(s, values):
        own = first + s
        first_is, second_is, third_is = (right_s[t, 0, s] == own for t in range(3))
        return (
            jnp.where(first_is, values[0], jnp.where(second_is, values[1], values[2])),
            jnp.where(first_is, values[1], values[0]),
            jnp.where(third_is, values[1], values[2]),
        )

    def left_indices(s):
        return by_term(s, [left_s[t, 0, s] for t in range(3)])

    def panel_block(pan, index):
        held = jnp.maximum(index, 0)
        owner = lax.div(held, SLOTS)
        near = lax.rem(owner - c + 1 + COLS, COLS)
        place = jnp.minimum(near * SLOTS + held - owner * SLOTS, 3 * SLOTS)
        return pan[jnp.where(index >= 0, place, 3 * SLOTS)]

    def left_blocks(pan, s):
        return left_operand([panel_block(pan, index) for index in left_indices(s)])

    def mirror_tables():
        threes = jnp.int32(0)
        table = jnp.zeros((1, BS), jnp.int32)
        to_up, to_down = table, table
        ups, downs = jnp.int32(0), jnp.int32(0)
        for s in range(SLOTS):
            self_left, *others = left_indices(s)
            diagonal = self_left == c * SLOTS + s
            three = jnp.logical_and(jnp.logical_not(diagonal), others[1] >= 0)
            threes = threes + three.astype(jnp.int32)
            for u, index in enumerate(others):
                e = 2 * s + u
                side = lax.rem(lax.div(jnp.maximum(index, 0), SLOTS) - c + COLS, COLS)
                live = jnp.logical_and(diagonal, index >= 0)
                is_up = jnp.logical_and(live, side == 1)
                is_down = jnp.logical_and(live, side == COLS - 1)
                rank = jnp.minimum(jnp.where(is_up, ups, downs), OFF_DIAG - 1)
                table = jnp.where(lane == e, rank, jnp.where(lane == TARGET + e, index, table))
                to_up = jnp.where(lane == jnp.where(is_up, ups, -1), place_s[e], to_up)
                to_down = jnp.where(lane == jnp.where(is_down, downs, -1), place_s[e], to_down)
                ups, downs = ups + is_up.astype(jnp.int32), downs + is_down.astype(jnp.int32)
        table_v[2] = table
        table_v[3] = to_up
        table_v[4] = to_down
        return threes

    def mirror(s):
        self_left = left_indices(s)[0]
        owner = lax.div(self_left, SLOTS)
        e = 2 * (self_left - owner * SLOTS)
        side = lax.rem(owner - c + COLS, COLS)
        row = jnp.where(side == COLS - 1, 0, jnp.where(side == 1, 1, 2))
        own = c * SLOTS + s
        e = e + (table_s[row, 0, TARGET + e + 1] == own).astype(jnp.int32)
        place = jnp.where(self_left == own, cap + s, place_s[e])
        near = mirror_in[jnp.where(row == 2, 0, row * OFF_DIAG + table_s[row, 0, e])]
        return jnp.where(row == 2, got_d[:, place].reshape(BS, BS), near)

    @pl.loop(1, ROWS)
    def _(step):
        dst = row_peer(step)
        want_copy(r, dst, dst).start()

    near_d = near_copies(0, own_d, pan_d)
    deal_out(0, own_d)
    for copy in near_d:
        copy.start()

    @pl.loop(1, ROWS)
    def _(step):
        src = row_peer(step)
        want_copy(src, r, src).wait_recv()

    to_smem = pltpu.make_async_copy(want_v, want_s, local_sem.at[5])
    to_smem.start()
    for load in loads[2:]:
        load.wait()
    threes = mirror_tables()
    over = jnp.where(jnp.logical_or(count > cap, threes > 0), 1.0, 0.0)
    for copy in table_copies:
        copy.start()
    to_smem.wait()

    deal_in(0)
    pass_on(0, 1, ROWS)
    deal_out(1, own_h)
    for copy in (*table_copies, *near_d):
        copy.wait_recv()
    tables_to_smem = pltpu.make_async_copy(table_v, table_s, local_sem.at[6])
    tables_to_smem.start()
    tables_to_smem.wait()
    get_in(0)
    for k in range(2):
        for q in range(OFF_DIAG):
            mirror_stage[k, q] = got_d[:, table_s[3 + k, 0, q]].reshape(BS, BS)
        mirror_copies[k].start()

    eye = lax.broadcasted_iota(jnp.int32, (BS, BS), 0) == lax.broadcasted_iota(jnp.int32, (BS, BS), 1)

    def trace_row(block, s):
        on = (left_indices(s)[0] == c * SLOTS + s).astype(jnp.float32)
        return jnp.sum(jnp.where(eye, block, 0.0), axis=0, keepdims=True) * on

    part[...] = jnp.zeros_like(part)

    @pl.loop(0, SLOTS, unroll=UNROLL)
    def _(s):
        square = product(left_blocks(pan_d, s), right_blocks(0, s))
        pan_q[SLOTS + s] = square
        own_q[s] = square
        part[0:1, :] += trace_row(own_d[s], s)
        part[1:2, :] += trace_row(square, s)

    def row_copy(src, dst, peer):
        return pltpu.make_async_remote_copy(
            src_ref=part, dst_ref=part_row.at[src], send_sem=row_send.at[dst], recv_sem=row_recv.at[src],
            device_id=(peer, c), device_id_type=MESH,
        )

    def col_copy(src, dst, peer):
        return pltpu.make_async_remote_copy(
            src_ref=part_col.at[src], dst_ref=part_col.at[src], send_sem=col_send.at[dst], recv_sem=col_recv.at[src],
            device_id=(r, peer), device_id_type=MESH,
        )

    def sum_rows_start():
        part[4:5, :] = jnp.zeros((1, BS), jnp.float32) + over

        @pl.loop(1, ROWS)
        def _(step):
            dst = row_peer(step)
            row_copy(r, dst, dst).start()

        part_row[r] = part[...]

    def sum_cols_start():
        @pl.loop(1, ROWS)
        def _(step):
            src = row_peer(step)
            row_copy(src, r, src).wait_recv()

        part_col[c] = jnp.sum(part_row[...], axis=0)

        @pl.loop(1, COLS)
        def _(step):
            dst = col_peer(step)
            col_copy(c, dst, dst).start()

    def trace_factors():
        @pl.loop(0, SLOTS, unroll=UNROLL)
        def _(s):
            square = own_q[s]
            turned = square.T
            self_left = left_indices(s)[0]
            corner = got_d[:, place_s[2 * s]].reshape(BS, BS)
            left = left_operand([square, panel_block(pan_d, self_left)])
            factor = product(left, right_operand([corner, square]))
            on = self_left == c * SLOTS + s
            turned_v[0, s] = turned
            turned_v[1, s] = jnp.where(on, 0.0, factor.T)
            part[3:4, :] += jnp.sum(jnp.where(on, turned * square, 0.0), axis=0, keepdims=True)

    def traces_without_triangles():
        @pl.loop(0, SLOTS, unroll=UNROLL)
        def _(s):
            back = mirror(s)
            part[2:3, :] += jnp.sum(turned_v[0, s] * back, axis=0, keepdims=True)
            part[3:4, :] += jnp.sum(turned_v[1, s] * back, axis=0, keepdims=True)

    def find_gamma():
        @pl.loop(1, COLS)
        def _(step):
            src = col_peer(step)
            col_copy(src, c, src).wait_recv()

        sums = jnp.sum(part_col[...], axis=0)
        over_ref[0, 0] = jnp.sum(sums[4:5, :])
        traces = jnp.sum(sums, axis=1, keepdims=True)
        one, two, three, four = (traces[k : k + 1, :] for k in range(4))
        trace_f = 4.0 * three - 3.0 * four
        trace_g = four - 2.0 * three + two
        return jnp.clip((one - trace_f) / jnp.maximum(jnp.abs(trace_g), 1.0), 0.0, 6.0)

    def make_cube():
        @pl.loop(0, SLOTS, unroll=UNROLL)
        def _(s):
            cube = product(left_blocks(pan_q, s), right_blocks(0, s))
            cube_v[s] = cube
            if not quick:
                part[2:3, :] += trace_row(cube, s)
                part[3:4, :] += jnp.sum(cube.T * mirror(s), axis=0, keepdims=True)

    def make_new(gamma):
        @pl.loop(0, SLOTS, unroll=UNROLL)
        def _(s):
            fourth = product(left_blocks(pan_q, s), right_blocks(2, s))
            cube = cube_v[s]
            new_ref[s] = 4.0 * cube - 3.0 * fourth + gamma * (fourth - 2.0 * cube + own_q[s])

    def make_energy():
        @pl.loop(0, SLOTS, unroll=UNROLL)
        def _(s):
            ew_ref[s] = product(left_blocks(pan_q, s), right_blocks(1, s))

    near_q = near_copies(1, own_q, pan_q)
    deal_out(2, own_q)
    for copy in near_q:
        copy.start()
    if quick:
        trace_factors()
        for copy in mirror_copies:
            copy.wait_recv()
        traces_without_triangles()
        sum_rows_start()
    deal_in(1)
    pass_on(1, 1, EARLY)
    deal_in(2)
    pass_on(2, 1, ROWS)
    pass_on(1, EARLY, ROWS)
    if quick:
        sum_cols_start()
    else:
        for copy in mirror_copies:
            copy.wait_recv()
    for copy in near_q:
        copy.wait_recv()
    make_cube()
    if not quick:
        sum_rows_start()
        sum_cols_start()
    gamma = find_gamma()
    if EARLY == ROWS:
        get_in(1)
        make_energy()
        get_in(2)
        make_new(gamma)
    else:
        get_in(2)
        make_new(gamma)
        get_in(1)
        make_energy()

    for copy in (*near_d, *near_q, *table_copies, *mirror_copies):
        copy.wait_send()

    @pl.loop(1, ROWS)
    def _(step):
        dst = row_peer(step)
        want_copy(r, dst, dst).wait_send()
        row_copy(r, dst, dst).wait_send()
        for k in range(3):
            deal_copy(k, r, dst, dst).wait_send()
            got_copy(k, r, dst, dst).wait_send()

    @pl.loop(1, COLS)
    def _(step):
        dst = col_peer(step)
        col_copy(c, dst, dst).wait_send()


def step(cap, dealt, quick, collective_id, *operands):
    any_space = pl.BlockSpec(memory_space=pl.ANY)
    smem = pl.BlockSpec(memory_space=pltpu.SMEM)
    vmem = pl.BlockSpec(memory_space=pltpu.VMEM)
    block = jax.ShapeDtypeStruct((SLOTS, BS, BS), jnp.float32)
    dma = pltpu.SemaphoreType.DMA
    panel = pltpu.VMEM((3 * SLOTS + 1, BS, BS), jnp.float32)
    own = pltpu.VMEM((SLOTS, BS, BS), jnp.float32)
    slices = pltpu.VMEM((ROWS * dealt, CUT, BS), jnp.float32)
    fetched = pltpu.VMEM((ROWS, cap + SLOTS, CUT, BS), jnp.float32)
    return pl.pallas_call(
        functools.partial(kernel, cap, dealt, quick),
        out_shape=(block, block, jax.ShapeDtypeStruct((1, 1), jnp.float32)),
        in_specs=[any_space] * 4,
        out_specs=(vmem, vmem, smem),
        scratch_shapes=[
            panel,
            panel,
            own,
            own,
            own,
            pltpu.VMEM((3, dealt, BS, BS), jnp.float32),
            slices,
            slices,
            slices,
            pltpu.VMEM((3, ROWS, cap, CUT, BS), jnp.float32),
            fetched,
            fetched,
            fetched,
            own,
            pltpu.VMEM((2, SLOTS, BS, BS), jnp.float32),
            pltpu.VMEM((2, OFF_DIAG, BS, BS), jnp.float32),
            pltpu.VMEM((2 * OFF_DIAG, BS, BS), jnp.float32),
            pltpu.SMEM((3, 1, SLOTS), jnp.int32),
            pltpu.SMEM((3, 1, SLOTS), jnp.int32),
            pltpu.SMEM((WANT_MOST,), jnp.int32),
            pltpu.VMEM((5, 1, BS), jnp.int32),
            pltpu.SMEM((5, 1, BS), jnp.int32),
            pltpu.VMEM((ROWS, 1, BS), jnp.int32),
            pltpu.SMEM((ROWS, 1, BS), jnp.int32),
            pltpu.VMEM((8, BS), jnp.float32),
            pltpu.VMEM((ROWS, 8, BS), jnp.float32),
            pltpu.VMEM((COLS, 8, BS), jnp.float32),
            dma((9,)),
            dma((2, 2)),
            dma((2, 2)),
            dma((3, ROWS)),
            dma((3, ROWS)),
            dma((3, ROWS)),
            dma((3, ROWS)),
            dma((ROWS,)),
            dma((ROWS,)),
            dma((ROWS,)),
            dma((ROWS,)),
            dma((COLS,)),
            dma((COLS,)),
            dma((2,)),
            dma((2,)),
            dma((2,)),
            dma((2,)),
        ],
        compiler_params=pltpu.CompilerParams(
            collective_id=collective_id, has_side_effects=True, vmem_limit_bytes=60 * 1024 * 1024
        ),
        cost_estimate=pl.CostEstimate(flops=2 * 9 * 4 * SLOTS * BS**3, bytes_accessed=5 * SLOTS * BS * BS, transcendentals=0),
    )(*operands)


def write_kernel(new_in, ew_in, new_ref, ew_ref, sem):
    pairs = ((new_in, new_ref), (ew_in, ew_ref))
    copies = [pltpu.make_async_copy(src, dst, sem.at[k]) for k, (src, dst) in enumerate(pairs)]
    for copy in copies:
        copy.start()
    for copy in copies:
        copy.wait()


def write_out(new, ew):
    any_space = pl.BlockSpec(memory_space=pl.ANY)
    block = jax.ShapeDtypeStruct((SLOTS, BS, BS), jnp.float32)
    return pl.pallas_call(
        write_kernel,
        out_shape=(block, block),
        in_specs=[any_space, any_space],
        out_specs=(any_space, any_space),
        scratch_shapes=[pltpu.SemaphoreType.DMA((2,))],
    )(new, ew)


def shards(density, hamiltonian, block_rows, block_cols, left_index, right_index):
    terms_first = (2, 0, 1)
    operands = (
        density[0], hamiltonian[0],
        jnp.transpose(left_index, terms_first), jnp.transpose(right_index, terms_first),
    )
    new, ew, over = step(WANT_FEW, min(WANT_FEW, SLOTS), True, 0, *operands)
    new, ew = lax.cond(
        over[0, 0] > 0.0,
        lambda new, ew, *operands: tuple(step(WANT_MOST, SLOTS, False, 1, *operands)[:2]),
        lambda new, ew, *operands: (new, ew),
        new, ew, *operands,
    )
    new, ew = write_out(new, ew)
    return new[None], ew[None]


def solution(mesh):
    in_specs = (
        P("row", "col", None, None),
        P("row", "col", None, None),
        P("row", "col"),
        P("row", "col"),
        P("row", "col", None),
        P("row", "col", None),
    )
    out_specs = (P("row", "col", None, None), P("row", "col", None, None))
    return jax.shard_map(shards, mesh=mesh, in_specs=in_specs, out_specs=out_specs, check_vma=False)
```

```python
import functools

import jax
import jax.numpy as jnp
from jax import lax
from jax.experimental import pallas as pl
from jax.experimental.pallas import tpu as pltpu
from jax.sharding import PartitionSpec as P

MESH = pl.DeviceIdType.MESH
ROWS = 16
COLS = 8
SLOTS = 10
BS = 128
CUT = BS // ROWS
OTHERS = 2
WANT_MOST = SLOTS * OTHERS
WANT_FEW = 8
OFF_DIAG = 6
TARGET = 32
UNROLL = 10
EARLY = ROWS
PLACES = 64


def halves(x):
    high = x.astype(jnp.bfloat16)
    low = (x - high.astype(jnp.float32)).astype(jnp.bfloat16)
    return high, low


def left_operand(blocks):
    pairs = [halves(block) for block in blocks]
    parts = [half for pair in pairs for half in pair] + [high for high, _ in pairs]
    return jnp.concatenate(parts, axis=1)


def right_operand(blocks):
    pairs = [halves(block) for block in blocks]
    parts = [high for high, _ in pairs for _ in range(2)] + [low for _, low in pairs]
    return jnp.concatenate(parts, axis=0)


def product(left, right):
    return jnp.dot(left, right, preferred_element_type=jnp.float32)


def kernel(
    cap, dealt, quick,
    d_ref, h_ref, left_ref, right_ref,
    new_ref, ew_ref, over_ref,
    pan_d, pan_q, own_d, own_h, own_q, pack, deal_d, deal_h, deal_q, stage, got_d, got_h, got_q, cube_v, turned_v,
    mirror_stage, mirror_in, left_s, right_s, place_s, table_v, table_s, want_v, want_s, part, part_row, part_col,
    local_sem, near_send, near_recv, deal_send, deal_recv, got_send, got_recv,
    want_send, want_recv, row_send, row_recv, col_send, col_recv, table_send, table_recv, mirror_send, mirror_recv,
):
    r, c = lax.axis_index("row"), lax.axis_index("col")
    up, down = lax.rem(c + 1, COLS), lax.rem(c + COLS - 1, COLS)
    first = r * SLOTS
    deal, got = (deal_d, deal_h, deal_q), (got_d, got_h, got_q)
    middle = pl.ds(SLOTS, SLOTS)

    def row_peer(step):
        return lax.rem(r + step, ROWS)

    def col_peer(step):
        return lax.rem(c + step, COLS)

    loads = [
        pltpu.make_async_copy(src, dst, local_sem.at[k])
        for k, (src, dst) in enumerate(
            (
                (right_ref, right_s),
                (d_ref, own_d),
                (d_ref, pan_d.at[middle]),
                (left_ref, left_s),
                (h_ref, own_h),
            )
        )
    ]
    for load in loads:
        load.start()

    barrier = pltpu.get_barrier_semaphore()

    @pl.loop(1, ROWS)
    def _(step):
        pl.semaphore_signal(barrier, inc=1, device_id=(row_peer(step), c), device_id_type=MESH)

    @pl.loop(1, COLS)
    def _(step):
        pl.semaphore_signal(barrier, inc=1, device_id=(r, col_peer(step)), device_id_type=MESH)

    loads[0].wait()

    lane = lax.broadcasted_iota(jnp.int32, (1, BS), 1)
    wanted = jnp.full((1, BS), PLACES, jnp.int32)
    count, packed = jnp.int32(0), jnp.int32(0)
    slots = [jnp.int32(p) for p in range(dealt)]
    for s in range(SLOTS):
        own = first + s
        one, two, three = (right_s[t, 0, s] for t in range(3))
        lone = True
        for u, index in enumerate((jnp.where(one == own, two, one), jnp.where(three == own, two, three))):
            live = index >= 0
            near = index - first
            here = jnp.logical_and(near >= 0, near < SLOTS)
            away = jnp.logical_and(live, jnp.logical_not(here))
            lone = jnp.logical_and(lone, jnp.logical_not(away))
            place_s[2 * s + u] = jnp.where(away, jnp.minimum(count, cap - 1), jnp.where(here, cap + near, 0))
            held = jnp.maximum(index, 0)
            owner = lax.div(held, SLOTS)
            address = owner * BS + PLACES + held - owner * SLOTS
            wanted = jnp.where(lane == jnp.where(away, count, -1), address, wanted)
            count = count + away.astype(jnp.int32)
        if dealt == SLOTS:
            wanted = jnp.where(lane == PLACES + s, r * dealt + s, wanted)
        else:
            wanted = jnp.where(lane == PLACES + s, r * dealt + jnp.minimum(packed, dealt - 1), wanted)
            here = jnp.where(lone, -1, packed)
            for p in range(min(s + 1, dealt)):
                slots[p] = jnp.where(here == p, s, slots[p])
            packed = packed + jnp.logical_not(lone).astype(jnp.int32)
    want_v[r] = wanted

    zero_block = jnp.zeros((BS, BS), jnp.float32)
    pan_d[3 * SLOTS] = zero_block
    pan_q[3 * SLOTS] = zero_block
    loads[1].wait()

    pl.semaphore_wait(barrier, ROWS + COLS - 2)

    def all_of(ref, count, send_sem, recv_sem):
        some = ref.at[pl.ds(0, count)]
        return pltpu.make_async_remote_copy(
            src_ref=some, dst_ref=some, send_sem=send_sem, recv_sem=recv_sem, device_id=(r, up), device_id_type=MESH
        )

    def all_wants():
        return all_of(want_v, ROWS - 1, want_send, want_recv)

    def all_dealt(k):
        return all_of(deal[k], (ROWS - 1) * dealt, deal_send.at[k], deal_recv.at[k])

    def all_got(k):
        return all_of(stage.at[k], ROWS - 1, got_send.at[k], got_recv.at[k])

    def all_rows():
        return all_of(part_row, ROWS - 1, row_send, row_recv)

    def all_cols():
        return all_of(part_col, COLS - 1, col_send, col_recv)

    def want_copy(src, dst, peer):
        return pltpu.make_async_remote_copy(
            src_ref=want_v.at[src], dst_ref=want_v.at[src], send_sem=want_send, recv_sem=want_recv,
            device_id=(peer, c), device_id_type=MESH,
        )

    def deal_copy(k, src, dst, peer):
        return pltpu.make_async_remote_copy(
            src_ref=pack.at[k, :, pl.ds(pl.multiple_of(dst * CUT, CUT), CUT), :],
            dst_ref=deal[k].at[pl.ds(src * dealt, dealt)],
            send_sem=deal_send.at[k], recv_sem=deal_recv.at[k],
            device_id=(peer, c), device_id_type=MESH,
        )

    def got_copy(k, src, dst, peer):
        return pltpu.make_async_remote_copy(
            src_ref=stage.at[k, dst], dst_ref=got[k].at[src, pl.ds(0, cap)],
            send_sem=got_send.at[k], recv_sem=got_recv.at[k],
            device_id=(peer, c), device_id_type=MESH,
        )

    def near_copies(k, own, pan):
        to_up = pltpu.make_async_remote_copy(
            src_ref=own, dst_ref=pan.at[pl.ds(0, SLOTS)],
            send_sem=near_send.at[k, 0], recv_sem=near_recv.at[k, 0],
            device_id=(r, up), device_id_type=MESH,
        )
        to_down = pltpu.make_async_remote_copy(
            src_ref=own, dst_ref=pan.at[pl.ds(2 * SLOTS, SLOTS)],
            send_sem=near_send.at[k, 1], recv_sem=near_recv.at[k, 1],
            device_id=(r, down), device_id_type=MESH,
        )
        return to_up, to_down

    table_copies = [
        pltpu.make_async_remote_copy(
            src_ref=table_v.at[2], dst_ref=table_v.at[k], send_sem=table_send.at[k], recv_sem=table_recv.at[k],
            device_id=(r, peer), device_id_type=MESH,
        )
        for k, peer in enumerate((up, down))
    ]
    mirror_copies = [
        pltpu.make_async_remote_copy(
            src_ref=mirror_stage.at[k], dst_ref=mirror_in.at[pl.ds(k * OFF_DIAG, OFF_DIAG)],
            send_sem=mirror_send.at[k], recv_sem=mirror_recv.at[k],
            device_id=(r, peer), device_id_type=MESH,
        )
        for k, peer in enumerate((up, down))
    ]

    def deal_out(k, own):
        for p in range(dealt):
            pack[k, p] = own[slots[p]]

        @pl.loop(1, ROWS)
        def _(step):
            dst = row_peer(step)
            deal_copy(k, r, dst, dst).start()

        mine = pl.ds(pl.multiple_of(r * CUT, CUT), CUT)
        for p in range(dealt):
            deal[k][r * dealt + p] = pack[k, p, mine, :]
        for s in range(SLOTS):
            got[k][:, cap + s] = own[s].reshape(ROWS, CUT, BS)

    def deal_in(k):
        all_dealt(k).wait_recv()

    def pick(k, dst, q):
        address = want_s[dst, 0, q]
        row = lax.div(address, BS)
        return deal[k][want_s[row, 0, address - row * BS]]

    def pass_on(k, low, high):
        @pl.loop(low, high)
        def _(step):
            dst = row_peer(step)
            for q in range(cap):
                stage[k, dst, q] = pick(k, dst, q)
            got_copy(k, r, dst, dst).start()

        if high == ROWS:
            for q in range(cap):
                got[k][r, q] = pick(k, r, q)

    def get_in(k):
        all_got(k).wait_recv()

    def right_blocks(k, s):
        places = (cap + s, place_s[2 * s], place_s[2 * s + 1])
        return right_operand([got[k][:, place].reshape(BS, BS) for place in places])

    def by_term(s, values):
        own = first + s
        first_is, second_is, third_is = (right_s[t, 0, s] == own for t in range(3))
        return (
            jnp.where(first_is, values[0], jnp.where(second_is, values[1], values[2])),
            jnp.where(first_is, values[1], values[0]),
            jnp.where(third_is, values[1], values[2]),
        )

    def left_indices(s):
        return by_term(s, [left_s[t, 0, s] for t in range(3)])

    def panel_block(pan, index):
        held = jnp.maximum(index, 0)
        owner = lax.div(held, SLOTS)
        near = lax.rem(owner - c + 1 + COLS, COLS)
        place = jnp.minimum(near * SLOTS + held - owner * SLOTS, 3 * SLOTS)
        return pan[jnp.where(index >= 0, place, 3 * SLOTS)]

    def left_blocks(pan, s):
        return left_operand([panel_block(pan, index) for index in left_indices(s)])

    def mirror_tables():
        threes = jnp.int32(0)
        table = jnp.zeros((1, BS), jnp.int32)
        to_up, to_down = table, table
        ups, downs = jnp.int32(0), jnp.int32(0)
        for s in range(SLOTS):
            self_left, *others = left_indices(s)
            diagonal = self_left == c * SLOTS + s
            three = jnp.logical_and(jnp.logical_not(diagonal), others[1] >= 0)
            threes = threes + three.astype(jnp.int32)
            for u, index in enumerate(others):
                e = 2 * s + u
                side = lax.rem(lax.div(jnp.maximum(index, 0), SLOTS) - c + COLS, COLS)
                live = jnp.logical_and(diagonal, index >= 0)
                is_up = jnp.logical_and(live, side == 1)
                is_down = jnp.logical_and(live, side == COLS - 1)
                rank = jnp.minimum(jnp.where(is_up, ups, downs), OFF_DIAG - 1)
                table = jnp.where(lane == e, rank, jnp.where(lane == TARGET + e, index, table))
                to_up = jnp.where(lane == jnp.where(is_up, ups, -1), place_s[e], to_up)
                to_down = jnp.where(lane == jnp.where(is_down, downs, -1), place_s[e], to_down)
                ups, downs = ups + is_up.astype(jnp.int32), downs + is_down.astype(jnp.int32)
        table_v[2] = table
        table_v[3] = to_up
        table_v[4] = to_down
        return threes

    def mirror(s):
        self_left = left_indices(s)[0]
        owner = lax.div(self_left, SLOTS)
        e = 2 * (self_left - owner * SLOTS)
        side = lax.rem(owner - c + COLS, COLS)
        row = jnp.where(side == COLS - 1, 0, jnp.where(side == 1, 1, 2))
        own = c * SLOTS + s
        e = e + (table_s[row, 0, TARGET + e + 1] == own).astype(jnp.int32)
        place = jnp.where(self_left == own, cap + s, place_s[e])
        near = mirror_in[jnp.where(row == 2, 0, row * OFF_DIAG + table_s[row, 0, e])]
        return jnp.where(row == 2, got_d[:, place].reshape(BS, BS), near)

    @pl.loop(1, ROWS)
    def _(step):
        dst = row_peer(step)
        want_copy(r, dst, dst).start()

    near_d = near_copies(0, own_d, pan_d)
    deal_out(0, own_d)
    for copy in near_d:
        copy.start()

    all_wants().wait_recv()
    to_smem = pltpu.make_async_copy(want_v, want_s, local_sem.at[5])
    to_smem.start()
    for load in loads[2:]:
        load.wait()
    threes = mirror_tables()
    over = jnp.where(jnp.logical_or(count > cap, threes > 0), 1.0, 0.0)
    for copy in table_copies:
        copy.start()
    to_smem.wait()

    deal_in(0)
    pass_on(0, 1, ROWS)
    deal_out(1, own_h)
    for copy in (*table_copies, *near_d):
        copy.wait_recv()
    tables_to_smem = pltpu.make_async_copy(table_v, table_s, local_sem.at[6])
    tables_to_smem.start()
    tables_to_smem.wait()
    get_in(0)
    for k in range(2):
        for q in range(OFF_DIAG):
            mirror_stage[k, q] = got_d[:, table_s[3 + k, 0, q]].reshape(BS, BS)
        mirror_copies[k].start()

    eye = lax.broadcasted_iota(jnp.int32, (BS, BS), 0) == lax.broadcasted_iota(jnp.int32, (BS, BS), 1)

    def trace_row(block, s):
        on = (left_indices(s)[0] == c * SLOTS + s).astype(jnp.float32)
        return jnp.sum(jnp.where(eye, block, 0.0), axis=0, keepdims=True) * on

    part[...] = jnp.zeros_like(part)

    @pl.loop(0, SLOTS, unroll=UNROLL)
    def _(s):
        square = product(left_blocks(pan_d, s), right_blocks(0, s))
        pan_q[SLOTS + s] = square
        own_q[s] = square
        part[0:1, :] += trace_row(own_d[s], s)
        part[1:2, :] += trace_row(square, s)

    def row_copy(src, dst, peer):
        return pltpu.make_async_remote_copy(
            src_ref=part, dst_ref=part_row.at[src], send_sem=row_send, recv_sem=row_recv,
            device_id=(peer, c), device_id_type=MESH,
        )

    def col_copy(src, dst, peer):
        return pltpu.make_async_remote_copy(
            src_ref=part_col.at[src], dst_ref=part_col.at[src], send_sem=col_send, recv_sem=col_recv,
            device_id=(r, peer), device_id_type=MESH,
        )

    def sum_rows_start():
        part[4:5, :] = jnp.zeros((1, BS), jnp.float32) + over

        @pl.loop(1, ROWS)
        def _(step):
            dst = row_peer(step)
            row_copy(r, dst, dst).start()

        part_row[r] = part[...]

    def sum_cols_start():
        all_rows().wait_recv()
        part_col[c] = jnp.sum(part_row[...], axis=0)

        @pl.loop(1, COLS)
        def _(step):
            dst = col_peer(step)
            col_copy(c, dst, dst).start()

    def trace_factors():
        @pl.loop(0, SLOTS, unroll=UNROLL)
        def _(s):
            square = own_q[s]
            turned = square.T
            self_left = left_indices(s)[0]
            corner = got_d[:, place_s[2 * s]].reshape(BS, BS)
            left = left_operand([square, panel_block(pan_d, self_left)])
            factor = product(left, right_operand([corner, square]))
            on = self_left == c * SLOTS + s
            turned_v[0, s] = turned
            turned_v[1, s] = jnp.where(on, 0.0, factor.T)
            part[3:4, :] += jnp.sum(jnp.where(on, turned * square, 0.0), axis=0, keepdims=True)

    def traces_without_triangles():
        @pl.loop(0, SLOTS, unroll=UNROLL)
        def _(s):
            back = mirror(s)
            part[2:3, :] += jnp.sum(turned_v[0, s] * back, axis=0, keepdims=True)
            part[3:4, :] += jnp.sum(turned_v[1, s] * back, axis=0, keepdims=True)

    def find_gamma():
        all_cols().wait_recv()
        sums = jnp.sum(part_col[...], axis=0)
        over_ref[0, 0] = jnp.sum(sums[4:5, :])
        traces = jnp.sum(sums, axis=1, keepdims=True)
        one, two, three, four = (traces[k : k + 1, :] for k in range(4))
        trace_f = 4.0 * three - 3.0 * four
        trace_g = four - 2.0 * three + two
        return jnp.clip((one - trace_f) / jnp.maximum(jnp.abs(trace_g), 1.0), 0.0, 6.0)

    def make_cube():
        @pl.loop(0, SLOTS, unroll=UNROLL)
        def _(s):
            cube = product(left_blocks(pan_q, s), right_blocks(0, s))
            cube_v[s] = cube
            if not quick:
                part[2:3, :] += trace_row(cube, s)
                part[3:4, :] += jnp.sum(cube.T * mirror(s), axis=0, keepdims=True)

    def make_new(gamma):
        @pl.loop(0, SLOTS, unroll=UNROLL)
        def _(s):
            fourth = product(left_blocks(pan_q, s), right_blocks(2, s))
            cube = cube_v[s]
            new_ref[s] = 4.0 * cube - 3.0 * fourth + gamma * (fourth - 2.0 * cube + own_q[s])

    def make_energy():
        @pl.loop(0, SLOTS, unroll=UNROLL)
        def _(s):
            ew_ref[s] = product(left_blocks(pan_q, s), right_blocks(1, s))

    near_q = near_copies(1, own_q, pan_q)
    deal_out(2, own_q)
    for copy in near_q:
        copy.start()
    if quick:
        trace_factors()
        for copy in mirror_copies:
            copy.wait_recv()
        traces_without_triangles()
        sum_rows_start()
    deal_in(1)
    pass_on(1, 1, EARLY)
    deal_in(2)
    pass_on(2, 1, ROWS)
    pass_on(1, EARLY, ROWS)
    if quick:
        sum_cols_start()
    else:
        for copy in mirror_copies:
            copy.wait_recv()
    for copy in near_q:
        copy.wait_recv()
    make_cube()
    if not quick:
        sum_rows_start()
        sum_cols_start()
    gamma = find_gamma()
    if EARLY == ROWS:
        get_in(1)
        make_energy()
        get_in(2)
        make_new(gamma)
    else:
        get_in(2)
        make_new(gamma)
        get_in(1)
        make_energy()

    for copy in (*near_d, *near_q, *table_copies, *mirror_copies):
        copy.wait_send()

    for copy in (all_wants(), all_rows(), all_cols()):
        copy.wait_send()
    for k in range(3):
        all_dealt(k).wait_send()
        all_got(k).wait_send()


def step(cap, dealt, quick, collective_id, *operands):
    any_space = pl.BlockSpec(memory_space=pl.ANY)
    smem = pl.BlockSpec(memory_space=pltpu.SMEM)
    vmem = pl.BlockSpec(memory_space=pltpu.VMEM)
    block = jax.ShapeDtypeStruct((SLOTS, BS, BS), jnp.float32)
    dma = pltpu.SemaphoreType.DMA
    panel = pltpu.VMEM((3 * SLOTS + 1, BS, BS), jnp.float32)
    own = pltpu.VMEM((SLOTS, BS, BS), jnp.float32)
    slices = pltpu.VMEM((ROWS * dealt, CUT, BS), jnp.float32)
    fetched = pltpu.VMEM((ROWS, cap + SLOTS, CUT, BS), jnp.float32)
    return pl.pallas_call(
        functools.partial(kernel, cap, dealt, quick),
        out_shape=(block, block, jax.ShapeDtypeStruct((1, 1), jnp.float32)),
        in_specs=[any_space] * 4,
        out_specs=(vmem, vmem, smem),
        scratch_shapes=[
            panel,
            panel,
            own,
            own,
            own,
            pltpu.VMEM((3, dealt, BS, BS), jnp.float32),
            slices,
            slices,
            slices,
            pltpu.VMEM((3, ROWS, cap, CUT, BS), jnp.float32),
            fetched,
            fetched,
            fetched,
            own,
            pltpu.VMEM((2, SLOTS, BS, BS), jnp.float32),
            pltpu.VMEM((2, OFF_DIAG, BS, BS), jnp.float32),
            pltpu.VMEM((2 * OFF_DIAG, BS, BS), jnp.float32),
            pltpu.SMEM((3, 1, SLOTS), jnp.int32),
            pltpu.SMEM((3, 1, SLOTS), jnp.int32),
            pltpu.SMEM((WANT_MOST,), jnp.int32),
            pltpu.VMEM((5, 1, BS), jnp.int32),
            pltpu.SMEM((5, 1, BS), jnp.int32),
            pltpu.VMEM((ROWS, 1, BS), jnp.int32),
            pltpu.SMEM((ROWS, 1, BS), jnp.int32),
            pltpu.VMEM((8, BS), jnp.float32),
            pltpu.VMEM((ROWS, 8, BS), jnp.float32),
            pltpu.VMEM((COLS, 8, BS), jnp.float32),
            dma((9,)),
            dma((2, 2)),
            dma((2, 2)),
            dma((3,)),
            dma((3,)),
            dma((3,)),
            dma((3,)),
            dma,
            dma,
            dma,
            dma,
            dma,
            dma,
            dma((2,)),
            dma((2,)),
            dma((2,)),
            dma((2,)),
        ],
        compiler_params=pltpu.CompilerParams(
            collective_id=collective_id, has_side_effects=True, vmem_limit_bytes=60 * 1024 * 1024
        ),
        cost_estimate=pl.CostEstimate(flops=2 * 9 * 4 * SLOTS * BS**3, bytes_accessed=5 * SLOTS * BS * BS, transcendentals=0),
    )(*operands)


def write_kernel(new_in, ew_in, new_ref, ew_ref, sem):
    pairs = ((new_in, new_ref), (ew_in, ew_ref))
    copies = [pltpu.make_async_copy(src, dst, sem.at[k]) for k, (src, dst) in enumerate(pairs)]
    for copy in copies:
        copy.start()
    for copy in copies:
        copy.wait()


def write_out(new, ew):
    any_space = pl.BlockSpec(memory_space=pl.ANY)
    block = jax.ShapeDtypeStruct((SLOTS, BS, BS), jnp.float32)
    return pl.pallas_call(
        write_kernel,
        out_shape=(block, block),
        in_specs=[any_space, any_space],
        out_specs=(any_space, any_space),
        scratch_shapes=[pltpu.SemaphoreType.DMA((2,))],
    )(new, ew)


def shards(density, hamiltonian, block_rows, block_cols, left_index, right_index):
    terms_first = (2, 0, 1)
    operands = (
        density[0], hamiltonian[0],
        jnp.transpose(left_index, terms_first), jnp.transpose(right_index, terms_first),
    )
    new, ew, over = step(WANT_FEW, min(WANT_FEW, SLOTS), True, 0, *operands)
    new, ew = lax.cond(
        over[0, 0] > 0.0,
        lambda new, ew, *operands: tuple(step(WANT_MOST, SLOTS, False, 1, *operands)[:2]),
        lambda new, ew, *operands: (new, ew),
        new, ew, *operands,
    )
    new, ew = write_out(new, ew)
    return new[None], ew[None]


def solution(mesh):
    in_specs = (
        P("row", "col", None, None),
        P("row", "col", None, None),
        P("row", "col"),
        P("row", "col"),
        P("row", "col", None),
        P("row", "col", None),
    )
    out_specs = (P("row", "col", None, None), P("row", "col", None, None))
    return jax.shard_map(shards, mesh=mesh, in_specs=in_specs, out_specs=out_specs, check_vma=False)
```

```python
import functools

import jax
import jax.numpy as jnp
from jax import lax
from jax.experimental import pallas as pl
from jax.experimental.pallas import tpu as pltpu
from jax.sharding import PartitionSpec as P

MESH = pl.DeviceIdType.MESH
ROWS = 16
COLS = 8
SLOTS = 10
BS = 128
CUT = BS // ROWS
OTHERS = 2
WANT_MOST = SLOTS * OTHERS
WANT_FEW = 8
OFF_DIAG = 6
TARGET = 32
UNROLL = 10
EARLY = ROWS
PLACES = 64


def halves(x):
    high = x.astype(jnp.bfloat16)
    low = (x - high.astype(jnp.float32)).astype(jnp.bfloat16)
    return high, low


def left_operand(blocks):
    pairs = [halves(block) for block in blocks]
    parts = [half for pair in pairs for half in pair] + [high for high, _ in pairs]
    return jnp.concatenate(parts, axis=1)


def right_operand(blocks):
    pairs = [halves(block) for block in blocks]
    parts = [high for high, _ in pairs for _ in range(2)] + [low for _, low in pairs]
    return jnp.concatenate(parts, axis=0)


def product(left, right):
    return jnp.dot(left, right, preferred_element_type=jnp.float32)


def kernel(
    cap, dealt, quick,
    d_ref, h_ref, left_ref, right_ref,
    new_ref, ew_ref, over_ref,
    pan_d, pan_q, own_d, own_h, own_q, pack, deal_d, deal_h, deal_q, stage, got_d, got_h, got_q, cube_v, turned_v,
    mirror_stage, mirror_in, left_s, right_s, place_s, table_v, table_s, want_v, want_s, part, part_row, part_col,
    local_sem, near_send, near_recv, deal_send, deal_recv, got_send, got_recv,
    want_send, want_recv, row_send, row_recv, col_send, col_recv, table_send, table_recv, mirror_send, mirror_recv,
):
    r, c = lax.axis_index("row"), lax.axis_index("col")
    up, down = lax.rem(c + 1, COLS), lax.rem(c + COLS - 1, COLS)
    first = r * SLOTS
    deal, got = (deal_d, deal_h, deal_q), (got_d, got_h, got_q)
    middle = pl.ds(SLOTS, SLOTS)

    def row_peer(step):
        return lax.rem(r + step, ROWS)

    def col_peer(step):
        return lax.rem(c + step, COLS)

    loads = [
        pltpu.make_async_copy(src, dst, local_sem.at[k])
        for k, (src, dst) in enumerate(
            (
                (right_ref, right_s),
                (d_ref, own_d),
                (d_ref, pan_d.at[middle]),
                (left_ref, left_s),
                (h_ref, own_h),
            )
        )
    ]
    for load in loads:
        load.start()

    barrier = pltpu.get_barrier_semaphore()

    @pl.loop(1, ROWS, unroll=True)
    def _(step):
        pl.semaphore_signal(barrier, inc=1, device_id=(row_peer(step), c), device_id_type=MESH)

    @pl.loop(1, COLS, unroll=True)
    def _(step):
        pl.semaphore_signal(barrier, inc=1, device_id=(r, col_peer(step)), device_id_type=MESH)

    loads[0].wait()

    lane = lax.broadcasted_iota(jnp.int32, (1, BS), 1)
    wanted = jnp.full((1, BS), PLACES, jnp.int32)
    count, packed = jnp.int32(0), jnp.int32(0)
    slots = [jnp.int32(p) for p in range(dealt)]
    for s in range(SLOTS):
        own = first + s
        one, two, three = (right_s[t, 0, s] for t in range(3))
        lone = True
        for u, index in enumerate((jnp.where(one == own, two, one), jnp.where(three == own, two, three))):
            live = index >= 0
            near = index - first
            here = jnp.logical_and(near >= 0, near < SLOTS)
            away = jnp.logical_and(live, jnp.logical_not(here))
            lone = jnp.logical_and(lone, jnp.logical_not(away))
            place_s[2 * s + u] = jnp.where(away, jnp.minimum(count, cap - 1), jnp.where(here, cap + near, 0))
            held = jnp.maximum(index, 0)
            owner = lax.div(held, SLOTS)
            address = owner * BS + PLACES + held - owner * SLOTS
            wanted = jnp.where(lane == jnp.where(away, count, -1), address, wanted)
            count = count + away.astype(jnp.int32)
        if dealt == SLOTS:
            wanted = jnp.where(lane == PLACES + s, r * dealt + s, wanted)
        else:
            wanted = jnp.where(lane == PLACES + s, r * dealt + jnp.minimum(packed, dealt - 1), wanted)
            here = jnp.where(lone, -1, packed)
            for p in range(min(s + 1, dealt)):
                slots[p] = jnp.where(here == p, s, slots[p])
            packed = packed + jnp.logical_not(lone).astype(jnp.int32)
    want_v[r] = wanted

    zero_block = jnp.zeros((BS, BS), jnp.float32)
    pan_d[3 * SLOTS] = zero_block
    pan_q[3 * SLOTS] = zero_block
    loads[1].wait()

    pl.semaphore_wait(barrier, ROWS + COLS - 2)

    def all_of(ref, count, send_sem, recv_sem):
        some = ref.at[pl.ds(0, count)]
        return pltpu.make_async_remote_copy(
            src_ref=some, dst_ref=some, send_sem=send_sem, recv_sem=recv_sem, device_id=(r, up), device_id_type=MESH
        )

    def all_wants():
        return all_of(want_v, ROWS - 1, want_send, want_recv)

    def all_dealt(k):
        return all_of(deal[k], (ROWS - 1) * dealt, deal_send.at[k], deal_recv.at[k])

    def all_got(k):
        return all_of(stage.at[k], ROWS - 1, got_send.at[k], got_recv.at[k])

    def all_rows():
        return all_of(part_row, ROWS - 1, row_send, row_recv)

    def all_cols():
        return all_of(part_col, COLS - 1, col_send, col_recv)

    def want_copy(src, dst, peer):
        return pltpu.make_async_remote_copy(
            src_ref=want_v.at[src], dst_ref=want_v.at[src], send_sem=want_send, recv_sem=want_recv,
            device_id=(peer, c), device_id_type=MESH,
        )

    def deal_copy(k, src, dst, peer):
        return pltpu.make_async_remote_copy(
            src_ref=pack.at[k, :, pl.ds(pl.multiple_of(dst * CUT, CUT), CUT), :],
            dst_ref=deal[k].at[pl.ds(src * dealt, dealt)],
            send_sem=deal_send.at[k], recv_sem=deal_recv.at[k],
            device_id=(peer, c), device_id_type=MESH,
        )

    def got_copy(k, src, dst, peer):
        return pltpu.make_async_remote_copy(
            src_ref=stage.at[k, dst], dst_ref=got[k].at[src, pl.ds(0, cap)],
            send_sem=got_send.at[k], recv_sem=got_recv.at[k],
            device_id=(peer, c), device_id_type=MESH,
        )

    def near_copies(k, own, pan):
        to_up = pltpu.make_async_remote_copy(
            src_ref=own, dst_ref=pan.at[pl.ds(0, SLOTS)],
            send_sem=near_send.at[k, 0], recv_sem=near_recv.at[k, 0],
            device_id=(r, up), device_id_type=MESH,
        )
        to_down = pltpu.make_async_remote_copy(
            src_ref=own, dst_ref=pan.at[pl.ds(2 * SLOTS, SLOTS)],
            send_sem=near_send.at[k, 1], recv_sem=near_recv.at[k, 1],
            device_id=(r, down), device_id_type=MESH,
        )
        return to_up, to_down

    table_copies = [
        pltpu.make_async_remote_copy(
            src_ref=table_v.at[2], dst_ref=table_v.at[k], send_sem=table_send.at[k], recv_sem=table_recv.at[k],
            device_id=(r, peer), device_id_type=MESH,
        )
        for k, peer in enumerate((up, down))
    ]
    mirror_copies = [
        pltpu.make_async_remote_copy(
            src_ref=mirror_stage.at[k], dst_ref=mirror_in.at[pl.ds(k * OFF_DIAG, OFF_DIAG)],
            send_sem=mirror_send.at[k], recv_sem=mirror_recv.at[k],
            device_id=(r, peer), device_id_type=MESH,
        )
        for k, peer in enumerate((up, down))
    ]

    def deal_out(k, own):
        for p in range(dealt):
            pack[k, p] = own[slots[p]]

        @pl.loop(1, ROWS, unroll=True)
        def _(step):
            dst = row_peer(step)
            deal_copy(k, r, dst, dst).start()

        mine = pl.ds(pl.multiple_of(r * CUT, CUT), CUT)
        for p in range(dealt):
            deal[k][r * dealt + p] = pack[k, p, mine, :]
        for s in range(SLOTS):
            got[k][:, cap + s] = own[s].reshape(ROWS, CUT, BS)

    def deal_in(k):
        all_dealt(k).wait_recv()

    def pick(k, dst, q):
        address = want_s[dst, 0, q]
        row = lax.div(address, BS)
        return deal[k][want_s[row, 0, address - row * BS]]

    def pass_on(k, low, high):
        @pl.loop(low, high)
        def _(step):
            dst = row_peer(step)
            for q in range(cap):
                stage[k, dst, q] = pick(k, dst, q)
            got_copy(k, r, dst, dst).start()

        if high == ROWS:
            for q in range(cap):
                got[k][r, q] = pick(k, r, q)

    def get_in(k):
        all_got(k).wait_recv()

    def right_blocks(k, s):
        places = (cap + s, place_s[2 * s], place_s[2 * s + 1])
        return right_operand([got[k][:, place].reshape(BS, BS) for place in places])

    def by_term(s, values):
        own = first + s
        first_is, second_is, third_is = (right_s[t, 0, s] == own for t in range(3))
        return (
            jnp.where(first_is, values[0], jnp.where(second_is, values[1], values[2])),
            jnp.where(first_is, values[1], values[0]),
            jnp.where(third_is, values[1], values[2]),
        )

    def left_indices(s):
        return by_term(s, [left_s[t, 0, s] for t in range(3)])

    def panel_block(pan, index):
        held = jnp.maximum(index, 0)
        owner = lax.div(held, SLOTS)
        near = lax.rem(owner - c + 1 + COLS, COLS)
        place = jnp.minimum(near * SLOTS + held - owner * SLOTS, 3 * SLOTS)
        return pan[jnp.where(index >= 0, place, 3 * SLOTS)]

    def left_blocks(pan, s):
        return left_operand([panel_block(pan, index) for index in left_indices(s)])

    def mirror_tables():
        threes = jnp.int32(0)
        table = jnp.zeros((1, BS), jnp.int32)
        to_up, to_down = table, table
        ups, downs = jnp.int32(0), jnp.int32(0)
        for s in range(SLOTS):
            self_left, *others = left_indices(s)
            diagonal = self_left == c * SLOTS + s
            three = jnp.logical_and(jnp.logical_not(diagonal), others[1] >= 0)
            threes = threes + three.astype(jnp.int32)
            for u, index in enumerate(others):
                e = 2 * s + u
                side = lax.rem(lax.div(jnp.maximum(index, 0), SLOTS) - c + COLS, COLS)
                live = jnp.logical_and(diagonal, index >= 0)
                is_up = jnp.logical_and(live, side == 1)
                is_down = jnp.logical_and(live, side == COLS - 1)
                rank = jnp.minimum(jnp.where(is_up, ups, downs), OFF_DIAG - 1)
                table = jnp.where(lane == e, rank, jnp.where(lane == TARGET + e, index, table))
                to_up = jnp.where(lane == jnp.where(is_up, ups, -1), place_s[e], to_up)
                to_down = jnp.where(lane == jnp.where(is_down, downs, -1), place_s[e], to_down)
                ups, downs = ups + is_up.astype(jnp.int32), downs + is_down.astype(jnp.int32)
        table_v[2] = table
        table_v[3] = to_up
        table_v[4] = to_down
        return threes

    def mirror(s):
        self_left = left_indices(s)[0]
        owner = lax.div(self_left, SLOTS)
        e = 2 * (self_left - owner * SLOTS)
        side = lax.rem(owner - c + COLS, COLS)
        row = jnp.where(side == COLS - 1, 0, jnp.where(side == 1, 1, 2))
        own = c * SLOTS + s
        e = e + (table_s[row, 0, TARGET + e + 1] == own).astype(jnp.int32)
        place = jnp.where(self_left == own, cap + s, place_s[e])
        near = mirror_in[jnp.where(row == 2, 0, row * OFF_DIAG + table_s[row, 0, e])]
        return jnp.where(row == 2, got_d[:, place].reshape(BS, BS), near)

    @pl.loop(1, ROWS, unroll=True)
    def _(step):
        dst = row_peer(step)
        want_copy(r, dst, dst).start()

    near_d = near_copies(0, own_d, pan_d)
    deal_out(0, own_d)
    for copy in near_d:
        copy.start()

    all_wants().wait_recv()
    to_smem = pltpu.make_async_copy(want_v, want_s, local_sem.at[5])
    to_smem.start()
    for load in loads[2:]:
        load.wait()
    threes = mirror_tables()
    over = jnp.where(jnp.logical_or(count > cap, threes > 0), 1.0, 0.0)
    for copy in table_copies:
        copy.start()
    to_smem.wait()

    deal_in(0)
    pass_on(0, 1, ROWS)
    deal_out(1, own_h)
    for copy in (*table_copies, *near_d):
        copy.wait_recv()
    tables_to_smem = pltpu.make_async_copy(table_v, table_s, local_sem.at[6])
    tables_to_smem.start()
    tables_to_smem.wait()
    get_in(0)
    for k in range(2):
        for q in range(OFF_DIAG):
            mirror_stage[k, q] = got_d[:, table_s[3 + k, 0, q]].reshape(BS, BS)
        mirror_copies[k].start()

    eye = lax.broadcasted_iota(jnp.int32, (BS, BS), 0) == lax.broadcasted_iota(jnp.int32, (BS, BS), 1)

    def trace_row(block, s):
        on = (left_indices(s)[0] == c * SLOTS + s).astype(jnp.float32)
        return jnp.sum(jnp.where(eye, block, 0.0), axis=0, keepdims=True) * on

    part[...] = jnp.zeros_like(part)

    @pl.loop(0, SLOTS, unroll=UNROLL)
    def _(s):
        square = product(left_blocks(pan_d, s), right_blocks(0, s))
        pan_q[SLOTS + s] = square
        own_q[s] = square
        part[0:1, :] += trace_row(own_d[s], s)
        part[1:2, :] += trace_row(square, s)

    def row_copy(src, dst, peer):
        return pltpu.make_async_remote_copy(
            src_ref=part, dst_ref=part_row.at[src], send_sem=row_send, recv_sem=row_recv,
            device_id=(peer, c), device_id_type=MESH,
        )

    def col_copy(src, dst, peer):
        return pltpu.make_async_remote_copy(
            src_ref=part_col.at[src], dst_ref=part_col.at[src], send_sem=col_send, recv_sem=col_recv,
            device_id=(r, peer), device_id_type=MESH,
        )

    def sum_rows_start():
        part[4:5, :] = jnp.zeros((1, BS), jnp.float32) + over

        @pl.loop(1, ROWS, unroll=True)
        def _(step):
            dst = row_peer(step)
            row_copy(r, dst, dst).start()

        part_row[r] = part[...]

    def sum_cols_start():
        all_rows().wait_recv()
        part_col[c] = jnp.sum(part_row[...], axis=0)

        @pl.loop(1, COLS, unroll=True)
        def _(step):
            dst = col_peer(step)
            col_copy(c, dst, dst).start()

    def trace_factors():
        @pl.loop(0, SLOTS, unroll=UNROLL)
        def _(s):
            square = own_q[s]
            turned = square.T
            self_left = left_indices(s)[0]
            corner = got_d[:, place_s[2 * s]].reshape(BS, BS)
            left = left_operand([square, panel_block(pan_d, self_left)])
            factor = product(left, right_operand([corner, square]))
            on = self_left == c * SLOTS + s
            turned_v[0, s] = turned
            turned_v[1, s] = jnp.where(on, 0.0, factor.T)
            part[3:4, :] += jnp.sum(jnp.where(on, turned * square, 0.0), axis=0, keepdims=True)

    def traces_without_triangles():
        @pl.loop(0, SLOTS, unroll=UNROLL)
        def _(s):
            back = mirror(s)
            part[2:3, :] += jnp.sum(turned_v[0, s] * back, axis=0, keepdims=True)
            part[3:4, :] += jnp.sum(turned_v[1, s] * back, axis=0, keepdims=True)

    def find_gamma():
        all_cols().wait_recv()
        sums = jnp.sum(part_col[...], axis=0)
        over_ref[0, 0] = jnp.sum(sums[4:5, :])
        traces = jnp.sum(sums, axis=1, keepdims=True)
        one, two, three, four = (traces[k : k + 1, :] for k in range(4))
        trace_f = 4.0 * three - 3.0 * four
        trace_g = four - 2.0 * three + two
        return jnp.clip((one - trace_f) / jnp.maximum(jnp.abs(trace_g), 1.0), 0.0, 6.0)

    def make_cube():
        @pl.loop(0, SLOTS, unroll=UNROLL)
        def _(s):
            cube = product(left_blocks(pan_q, s), right_blocks(0, s))
            cube_v[s] = cube
            if not quick:
                part[2:3, :] += trace_row(cube, s)
                part[3:4, :] += jnp.sum(cube.T * mirror(s), axis=0, keepdims=True)

    def make_new(gamma):
        @pl.loop(0, SLOTS, unroll=UNROLL)
        def _(s):
            fourth = product(left_blocks(pan_q, s), right_blocks(2, s))
            cube = cube_v[s]
            new_ref[s] = 4.0 * cube - 3.0 * fourth + gamma * (fourth - 2.0 * cube + own_q[s])

    def make_energy():
        @pl.loop(0, SLOTS, unroll=UNROLL)
        def _(s):
            ew_ref[s] = product(left_blocks(pan_q, s), right_blocks(1, s))

    near_q = near_copies(1, own_q, pan_q)
    deal_out(2, own_q)
    for copy in near_q:
        copy.start()
    if quick:
        trace_factors()
        for copy in mirror_copies:
            copy.wait_recv()
        traces_without_triangles()
        sum_rows_start()
    deal_in(1)
    pass_on(1, 1, EARLY)
    deal_in(2)
    pass_on(2, 1, ROWS)
    pass_on(1, EARLY, ROWS)
    if quick:
        sum_cols_start()
    else:
        for copy in mirror_copies:
            copy.wait_recv()
    for copy in near_q:
        copy.wait_recv()
    make_cube()
    if not quick:
        sum_rows_start()
        sum_cols_start()
    gamma = find_gamma()
    if EARLY == ROWS:
        get_in(1)
        make_energy()
        get_in(2)
        make_new(gamma)
    else:
        get_in(2)
        make_new(gamma)
        get_in(1)
        make_energy()

    for copy in (*near_d, *near_q, *table_copies, *mirror_copies):
        copy.wait_send()

    for copy in (all_wants(), all_rows(), all_cols()):
        copy.wait_send()
    for k in range(3):
        all_dealt(k).wait_send()
        all_got(k).wait_send()


def step(cap, dealt, quick, collective_id, *operands):
    any_space = pl.BlockSpec(memory_space=pl.ANY)
    smem = pl.BlockSpec(memory_space=pltpu.SMEM)
    vmem = pl.BlockSpec(memory_space=pltpu.VMEM)
    block = jax.ShapeDtypeStruct((SLOTS, BS, BS), jnp.float32)
    dma = pltpu.SemaphoreType.DMA
    panel = pltpu.VMEM((3 * SLOTS + 1, BS, BS), jnp.float32)
    own = pltpu.VMEM((SLOTS, BS, BS), jnp.float32)
    slices = pltpu.VMEM((ROWS * dealt, CUT, BS), jnp.float32)
    fetched = pltpu.VMEM((ROWS, cap + SLOTS, CUT, BS), jnp.float32)
    return pl.pallas_call(
        functools.partial(kernel, cap, dealt, quick),
        out_shape=(block, block, jax.ShapeDtypeStruct((1, 1), jnp.float32)),
        in_specs=[any_space] * 4,
        out_specs=(vmem, vmem, smem),
        scratch_shapes=[
            panel,
            panel,
            own,
            own,
            own,
            pltpu.VMEM((3, dealt, BS, BS), jnp.float32),
            slices,
            slices,
            slices,
            pltpu.VMEM((3, ROWS, cap, CUT, BS), jnp.float32),
            fetched,
            fetched,
            fetched,
            own,
            pltpu.VMEM((2, SLOTS, BS, BS), jnp.float32),
            pltpu.VMEM((2, OFF_DIAG, BS, BS), jnp.float32),
            pltpu.VMEM((2 * OFF_DIAG, BS, BS), jnp.float32),
            pltpu.SMEM((3, 1, SLOTS), jnp.int32),
            pltpu.SMEM((3, 1, SLOTS), jnp.int32),
            pltpu.SMEM((WANT_MOST,), jnp.int32),
            pltpu.VMEM((5, 1, BS), jnp.int32),
            pltpu.SMEM((5, 1, BS), jnp.int32),
            pltpu.VMEM((ROWS, 1, BS), jnp.int32),
            pltpu.SMEM((ROWS, 1, BS), jnp.int32),
            pltpu.VMEM((8, BS), jnp.float32),
            pltpu.VMEM((ROWS, 8, BS), jnp.float32),
            pltpu.VMEM((COLS, 8, BS), jnp.float32),
            dma((9,)),
            dma((2, 2)),
            dma((2, 2)),
            dma((3,)),
            dma((3,)),
            dma((3,)),
            dma((3,)),
            dma,
            dma,
            dma,
            dma,
            dma,
            dma,
            dma((2,)),
            dma((2,)),
            dma((2,)),
            dma((2,)),
        ],
        compiler_params=pltpu.CompilerParams(
            collective_id=collective_id, has_side_effects=True, vmem_limit_bytes=60 * 1024 * 1024
        ),
        cost_estimate=pl.CostEstimate(flops=2 * 9 * 4 * SLOTS * BS**3, bytes_accessed=5 * SLOTS * BS * BS, transcendentals=0),
    )(*operands)


def write_kernel(new_in, ew_in, new_ref, ew_ref, sem):
    pairs = ((new_in, new_ref), (ew_in, ew_ref))
    copies = [pltpu.make_async_copy(src, dst, sem.at[k]) for k, (src, dst) in enumerate(pairs)]
    for copy in copies:
        copy.start()
    for copy in copies:
        copy.wait()


def write_out(new, ew):
    any_space = pl.BlockSpec(memory_space=pl.ANY)
    block = jax.ShapeDtypeStruct((SLOTS, BS, BS), jnp.float32)
    return pl.pallas_call(
        write_kernel,
        out_shape=(block, block),
        in_specs=[any_space, any_space],
        out_specs=(any_space, any_space),
        scratch_shapes=[pltpu.SemaphoreType.DMA((2,))],
    )(new, ew)


def shards(density, hamiltonian, block_rows, block_cols, left_index, right_index):
    terms_first = (2, 0, 1)
    operands = (
        density[0], hamiltonian[0],
        jnp.transpose(left_index, terms_first), jnp.transpose(right_index, terms_first),
    )
    new, ew, over = step(WANT_FEW, min(WANT_FEW, SLOTS), True, 0, *operands)
    new, ew = lax.cond(
        over[0, 0] > 0.0,
        lambda new, ew, *operands: tuple(step(WANT_MOST, SLOTS, False, 1, *operands)[:2]),
        lambda new, ew, *operands: (new, ew),
        new, ew, *operands,
    )
    new, ew = write_out(new, ew)
    return new[None], ew[None]


def solution(mesh):
    in_specs = (
        P("row", "col", None, None),
        P("row", "col", None, None),
        P("row", "col"),
        P("row", "col"),
        P("row", "col", None),
        P("row", "col", None),
    )
    out_specs = (P("row", "col", None, None), P("row", "col", None, None))
    return jax.shard_map(shards, mesh=mesh, in_specs=in_specs, out_specs=out_specs, check_vma=False)
```

```python
import functools

import jax
import jax.numpy as jnp
from jax import lax
from jax.experimental import pallas as pl
from jax.experimental.pallas import tpu as pltpu
from jax.sharding import PartitionSpec as P

MESH = pl.DeviceIdType.MESH
ROWS = 16
COLS = 8
SLOTS = 10
BS = 128
CUT = BS // ROWS
OTHERS = 2
WANT_MOST = SLOTS * OTHERS
WANT_FEW = 8
OFF_DIAG = 6
TARGET = 32
UNROLL = 10
EARLY = ROWS
PLACES = 64


def halves(x):
    high = x.astype(jnp.bfloat16)
    low = (x - high.astype(jnp.float32)).astype(jnp.bfloat16)
    return high, low


def left_operand(blocks):
    pairs = [halves(block) for block in blocks]
    parts = [half for pair in pairs for half in pair] + [high for high, _ in pairs]
    return jnp.concatenate(parts, axis=1)


def right_operand(blocks):
    pairs = [halves(block) for block in blocks]
    parts = [high for high, _ in pairs for _ in range(2)] + [low for _, low in pairs]
    return jnp.concatenate(parts, axis=0)


def product(left, right):
    return jnp.dot(left, right, preferred_element_type=jnp.float32)


def kernel(
    cap, dealt, quick,
    d_ref, h_ref, left_ref, right_ref,
    new_ref, ew_ref, over_ref,
    pan_d, pan_q, own_d, own_h, own_q, pack, deal_d, deal_h, deal_q, stage, got_d, got_h, got_q, cube_v, turned_v,
    mirror_stage, mirror_in, left_s, right_s, place_s, table_v, table_s, want_v, want_s, part, part_row, part_col,
    local_sem, near_send, near_recv, deal_send, deal_recv, got_send, got_recv,
    want_send, want_recv, row_send, row_recv, col_send, col_recv, table_send, table_recv, mirror_send, mirror_recv,
):
    r, c = lax.axis_index("row"), lax.axis_index("col")
    up, down = lax.rem(c + 1, COLS), lax.rem(c + COLS - 1, COLS)
    first = r * SLOTS
    deal, got = (deal_d, deal_h, deal_q), (got_d, got_h, got_q)
    middle = pl.ds(SLOTS, SLOTS)

    def row_peer(step):
        return lax.rem(r + step, ROWS)

    def col_peer(step):
        return lax.rem(c + step, COLS)

    loads = [
        pltpu.make_async_copy(src, dst, local_sem.at[k])
        for k, (src, dst) in enumerate(
            (
                (right_ref, right_s),
                (d_ref, own_d),
                (d_ref, pan_d.at[middle]),
                (left_ref, left_s),
                (h_ref, own_h),
            )
        )
    ]
    for load in loads:
        load.start()

    barrier = pltpu.get_barrier_semaphore()

    @pl.loop(1, ROWS, unroll=True)
    def _(step):
        pl.semaphore_signal(barrier, inc=1, device_id=(row_peer(step), c), device_id_type=MESH)

    @pl.loop(1, COLS, unroll=True)
    def _(step):
        pl.semaphore_signal(barrier, inc=1, device_id=(r, col_peer(step)), device_id_type=MESH)

    loads[0].wait()

    lane = lax.broadcasted_iota(jnp.int32, (1, BS), 1)
    wanted = jnp.full((1, BS), PLACES, jnp.int32)
    count, packed = jnp.int32(0), jnp.int32(0)
    slots = [jnp.int32(p) for p in range(dealt)]
    for s in range(SLOTS):
        own = first + s
        one, two, three = (right_s[t, 0, s] for t in range(3))
        lone = True
        for u, index in enumerate((jnp.where(one == own, two, one), jnp.where(three == own, two, three))):
            live = index >= 0
            near = index - first
            here = jnp.logical_and(near >= 0, near < SLOTS)
            away = jnp.logical_and(live, jnp.logical_not(here))
            lone = jnp.logical_and(lone, jnp.logical_not(away))
            place_s[2 * s + u] = jnp.where(away, jnp.minimum(count, cap - 1), jnp.where(here, cap + near, 0))
            held = jnp.maximum(index, 0)
            owner = lax.div(held, SLOTS)
            address = owner * BS + PLACES + held - owner * SLOTS
            wanted = jnp.where(lane == jnp.where(away, count, -1), address, wanted)
            count = count + away.astype(jnp.int32)
        if dealt == SLOTS:
            wanted = jnp.where(lane == PLACES + s, r * dealt + s, wanted)
        else:
            wanted = jnp.where(lane == PLACES + s, r * dealt + jnp.minimum(packed, dealt - 1), wanted)
            here = jnp.where(lone, -1, packed)
            for p in range(min(s + 1, dealt)):
                slots[p] = jnp.where(here == p, s, slots[p])
            packed = packed + jnp.logical_not(lone).astype(jnp.int32)
    want_v[r] = wanted

    zero_block = jnp.zeros((BS, BS), jnp.float32)
    pan_d[3 * SLOTS] = zero_block
    pan_q[3 * SLOTS] = zero_block
    loads[1].wait()

    pl.semaphore_wait(barrier, ROWS + COLS - 2)

    def all_of(ref, count, send_sem, recv_sem):
        some = ref.at[pl.ds(0, count)]
        return pltpu.make_async_remote_copy(
            src_ref=some, dst_ref=some, send_sem=send_sem, recv_sem=recv_sem, device_id=(r, up), device_id_type=MESH
        )

    def all_wants():
        return all_of(want_v, ROWS - 1, want_send, want_recv)

    def all_dealt(k):
        return all_of(deal[k], (ROWS - 1) * dealt, deal_send.at[k], deal_recv.at[k])

    def all_got(k):
        return all_of(stage.at[k], ROWS - 1, got_send.at[k], got_recv.at[k])

    def all_rows():
        return all_of(part_row, ROWS - 1, row_send, row_recv)

    def all_cols():
        return all_of(part_col, COLS - 1, col_send, col_recv)

    def want_copy(src, dst, peer):
        return pltpu.make_async_remote_copy(
            src_ref=want_v.at[src], dst_ref=want_v.at[src], send_sem=want_send, recv_sem=want_recv,
            device_id=(peer, c), device_id_type=MESH,
        )

    def deal_copy(k, src, dst, peer):
        return pltpu.make_async_remote_copy(
            src_ref=pack.at[k, :, pl.ds(pl.multiple_of(dst * CUT, CUT), CUT), :],
            dst_ref=deal[k].at[pl.ds(src * dealt, dealt)],
            send_sem=deal_send.at[k], recv_sem=deal_recv.at[k],
            device_id=(peer, c), device_id_type=MESH,
        )

    def got_copy(k, src, dst, peer):
        return pltpu.make_async_remote_copy(
            src_ref=stage.at[k, dst], dst_ref=got[k].at[src, pl.ds(0, cap)],
            send_sem=got_send.at[k], recv_sem=got_recv.at[k],
            device_id=(peer, c), device_id_type=MESH,
        )

    def near_copies(k, own, pan):
        to_up = pltpu.make_async_remote_copy(
            src_ref=own, dst_ref=pan.at[pl.ds(0, SLOTS)],
            send_sem=near_send.at[k, 0], recv_sem=near_recv.at[k, 0],
            device_id=(r, up), device_id_type=MESH,
        )
        to_down = pltpu.make_async_remote_copy(
            src_ref=own, dst_ref=pan.at[pl.ds(2 * SLOTS, SLOTS)],
            send_sem=near_send.at[k, 1], recv_sem=near_recv.at[k, 1],
            device_id=(r, down), device_id_type=MESH,
        )
        return to_up, to_down

    table_copies = [
        pltpu.make_async_remote_copy(
            src_ref=table_v.at[2], dst_ref=table_v.at[k], send_sem=table_send.at[k], recv_sem=table_recv.at[k],
            device_id=(r, peer), device_id_type=MESH,
        )
        for k, peer in enumerate((up, down))
    ]
    mirror_copies = [
        pltpu.make_async_remote_copy(
            src_ref=mirror_stage.at[k], dst_ref=mirror_in.at[pl.ds(k * OFF_DIAG, OFF_DIAG)],
            send_sem=mirror_send.at[k], recv_sem=mirror_recv.at[k],
            device_id=(r, peer), device_id_type=MESH,
        )
        for k, peer in enumerate((up, down))
    ]

    def deal_out(k, own):
        for p in range(dealt):
            pack[k, p] = own[slots[p]]

        @pl.loop(1, ROWS, unroll=True)
        def _(step):
            dst = row_peer(step)
            deal_copy(k, r, dst, dst).start()

        mine = pl.ds(pl.multiple_of(r * CUT, CUT), CUT)
        for p in range(dealt):
            deal[k][r * dealt + p] = pack[k, p, mine, :]
        for s in range(SLOTS):
            got[k][:, cap + s] = own[s].reshape(ROWS, CUT, BS)

    def deal_in(k):
        all_dealt(k).wait_recv()

    def pick(k, dst, q):
        address = want_s[dst, 0, q]
        row = lax.div(address, BS)
        return deal[k][want_s[row, 0, address - row * BS]]

    def pass_on(k, low, high):
        @pl.loop(low, high)
        def _(step):
            dst = row_peer(step)
            for q in range(cap):
                stage[k, dst, q] = pick(k, dst, q)
            got_copy(k, r, dst, dst).start()

        if high == ROWS:
            for q in range(cap):
                got[k][r, q] = pick(k, r, q)

    def get_in(k):
        all_got(k).wait_recv()

    def right_blocks(k, s):
        places = (cap + s, place_s[2 * s], place_s[2 * s + 1])
        return right_operand([got[k][:, place].reshape(BS, BS) for place in places])

    def by_term(s, values):
        own = first + s
        first_is, second_is, third_is = (right_s[t, 0, s] == own for t in range(3))
        return (
            jnp.where(first_is, values[0], jnp.where(second_is, values[1], values[2])),
            jnp.where(first_is, values[1], values[0]),
            jnp.where(third_is, values[1], values[2]),
        )

    def left_indices(s):
        return by_term(s, [left_s[t, 0, s] for t in range(3)])

    def panel_block(pan, index):
        held = jnp.maximum(index, 0)
        owner = lax.div(held, SLOTS)
        near = lax.rem(owner - c + 1 + COLS, COLS)
        place = jnp.minimum(near * SLOTS + held - owner * SLOTS, 3 * SLOTS)
        return pan[jnp.where(index >= 0, place, 3 * SLOTS)]

    def left_blocks(pan, s):
        return left_operand([panel_block(pan, index) for index in left_indices(s)])

    def mirror_tables():
        threes = jnp.int32(0)
        table = jnp.zeros((1, BS), jnp.int32)
        to_up, to_down = table, table
        ups, downs = jnp.int32(0), jnp.int32(0)
        for s in range(SLOTS):
            self_left, *others = left_indices(s)
            diagonal = self_left == c * SLOTS + s
            three = jnp.logical_and(jnp.logical_not(diagonal), others[1] >= 0)
            threes = threes + three.astype(jnp.int32)
            for u, index in enumerate(others):
                e = 2 * s + u
                side = lax.rem(lax.div(jnp.maximum(index, 0), SLOTS) - c + COLS, COLS)
                live = jnp.logical_and(diagonal, index >= 0)
                is_up = jnp.logical_and(live, side == 1)
                is_down = jnp.logical_and(live, side == COLS - 1)
                rank = jnp.minimum(jnp.where(is_up, ups, downs), OFF_DIAG - 1)
                table = jnp.where(lane == e, rank, jnp.where(lane == TARGET + e, index, table))
                to_up = jnp.where(lane == jnp.where(is_up, ups, -1), place_s[e], to_up)
                to_down = jnp.where(lane == jnp.where(is_down, downs, -1), place_s[e], to_down)
                ups, downs = ups + is_up.astype(jnp.int32), downs + is_down.astype(jnp.int32)
        table_v[2] = table
        table_v[3] = to_up
        table_v[4] = to_down
        return threes

    def mirror(s):
        self_left = left_indices(s)[0]
        owner = lax.div(self_left, SLOTS)
        e = 2 * (self_left - owner * SLOTS)
        side = lax.rem(owner - c + COLS, COLS)
        row = jnp.where(side == COLS - 1, 0, jnp.where(side == 1, 1, 2))
        own = c * SLOTS + s
        e = e + (table_s[row, 0, TARGET + e + 1] == own).astype(jnp.int32)
        place = jnp.where(self_left == own, cap + s, place_s[e])
        near = mirror_in[jnp.where(row == 2, 0, row * OFF_DIAG + table_s[row, 0, e])]
        return jnp.where(row == 2, got_d[:, place].reshape(BS, BS), near)

    @pl.loop(1, ROWS, unroll=True)
    def _(step):
        dst = row_peer(step)
        want_copy(r, dst, dst).start()

    near_d = near_copies(0, own_d, pan_d)
    deal_out(0, own_d)
    for copy in near_d:
        copy.start()

    all_wants().wait_recv()
    to_smem = pltpu.make_async_copy(want_v, want_s, local_sem.at[5])
    to_smem.start()
    for load in loads[2:]:
        load.wait()
    threes = mirror_tables()
    over = jnp.where(jnp.logical_or(count > cap, threes > 0), 1.0, 0.0)
    for copy in table_copies:
        copy.start()
    to_smem.wait()

    deal_in(0)
    pass_on(0, 1, ROWS)
    deal_out(1, own_h)
    for copy in (*table_copies, *near_d):
        copy.wait_recv()
    tables_to_smem = pltpu.make_async_copy(table_v, table_s, local_sem.at[6])
    tables_to_smem.start()
    tables_to_smem.wait()
    get_in(0)
    for k in range(2):
        for q in range(OFF_DIAG):
            mirror_stage[k, q] = got_d[:, table_s[3 + k, 0, q]].reshape(BS, BS)
        mirror_copies[k].start()

    eye = lax.broadcasted_iota(jnp.int32, (BS, BS), 0) == lax.broadcasted_iota(jnp.int32, (BS, BS), 1)

    def trace_row(block, s):
        on = (left_indices(s)[0] == c * SLOTS + s).astype(jnp.float32)
        return jnp.sum(jnp.where(eye, block, 0.0), axis=0, keepdims=True) * on

    part[...] = jnp.zeros_like(part)

    @pl.loop(0, SLOTS, unroll=UNROLL)
    def _(s):
        square = product(left_blocks(pan_d, s), right_blocks(0, s))
        pan_q[SLOTS + s] = square
        own_q[s] = square
        part[0:1, :] += trace_row(own_d[s], s)
        part[1:2, :] += trace_row(square, s)

    def row_copy(src, dst, peer):
        return pltpu.make_async_remote_copy(
            src_ref=part, dst_ref=part_row.at[src], send_sem=row_send, recv_sem=row_recv,
            device_id=(peer, c), device_id_type=MESH,
        )

    def col_copy(src, dst, peer):
        return pltpu.make_async_remote_copy(
            src_ref=part_col.at[src], dst_ref=part_col.at[src], send_sem=col_send, recv_sem=col_recv,
            device_id=(r, peer), device_id_type=MESH,
        )

    def sum_rows_start():
        part[4:5, :] = jnp.zeros((1, BS), jnp.float32) + over

        @pl.loop(1, ROWS, unroll=True)
        def _(step):
            dst = row_peer(step)
            row_copy(r, dst, dst).start()

        part_row[r] = part[...]

    def sum_cols_start():
        all_rows().wait_recv()
        part_col[c] = jnp.sum(part_row[...], axis=0)

        @pl.loop(1, COLS, unroll=True)
        def _(step):
            dst = col_peer(step)
            col_copy(c, dst, dst).start()

    def trace_factors():
        @pl.loop(0, SLOTS, unroll=UNROLL)
        def _(s):
            square = own_q[s]
            turned = square.T
            self_left = left_indices(s)[0]
            corner = got_d[:, place_s[2 * s]].reshape(BS, BS)
            left = left_operand([square, panel_block(pan_d, self_left)])
            factor = product(left, right_operand([corner, square]))
            on = self_left == c * SLOTS + s
            turned_v[0, s] = turned
            turned_v[1, s] = jnp.where(on, 0.0, factor.T)
            part[3:4, :] += jnp.sum(jnp.where(on, turned * square, 0.0), axis=0, keepdims=True)

    def traces_without_triangles():
        @pl.loop(0, SLOTS, unroll=UNROLL)
        def _(s):
            back = mirror(s)
            part[2:3, :] += jnp.sum(turned_v[0, s] * back, axis=0, keepdims=True)
            part[3:4, :] += jnp.sum(turned_v[1, s] * back, axis=0, keepdims=True)

    def find_gamma():
        all_cols().wait_recv()
        sums = jnp.sum(part_col[...], axis=0)
        over_ref[0, 0] = jnp.sum(sums[4:5, :])
        traces = jnp.sum(sums, axis=1, keepdims=True)
        one, two, three, four = (traces[k : k + 1, :] for k in range(4))
        trace_f = 4.0 * three - 3.0 * four
        trace_g = four - 2.0 * three + two
        return jnp.clip((one - trace_f) / jnp.maximum(jnp.abs(trace_g), 1.0), 0.0, 6.0)

    def make_cube():
        @pl.loop(0, SLOTS, unroll=UNROLL)
        def _(s):
            cube = product(left_blocks(pan_q, s), right_blocks(0, s))
            cube_v[s] = cube
            if not quick:
                part[2:3, :] += trace_row(cube, s)
                part[3:4, :] += jnp.sum(cube.T * mirror(s), axis=0, keepdims=True)

    def make_new(gamma):
        @pl.loop(0, SLOTS, unroll=UNROLL)
        def _(s):
            fourth = product(left_blocks(pan_q, s), right_blocks(2, s))
            cube = cube_v[s]
            new_ref[s] = 4.0 * cube - 3.0 * fourth + gamma * (fourth - 2.0 * cube + own_q[s])

    def make_energy():
        @pl.loop(0, SLOTS, unroll=UNROLL)
        def _(s):
            ew_ref[s] = product(left_blocks(pan_q, s), right_blocks(1, s))

    near_q = near_copies(1, own_q, pan_q)
    deal_out(2, own_q)
    for copy in near_q:
        copy.start()
    if quick:
        trace_factors()
        for copy in mirror_copies:
            copy.wait_recv()
        traces_without_triangles()
        sum_rows_start()
    deal_in(1)
    pass_on(1, 1, EARLY)
    deal_in(2)
    pass_on(2, 1, ROWS)
    pass_on(1, EARLY, ROWS)
    if quick:
        sum_cols_start()
    else:
        for copy in mirror_copies:
            copy.wait_recv()
    for copy in near_q:
        copy.wait_recv()
    make_cube()
    if not quick:
        sum_rows_start()
        sum_cols_start()
    gamma = find_gamma()
    get_in(1)
    make_energy()
    for copy in (*near_d, *near_q, *table_copies, *mirror_copies, all_wants(), all_rows(), all_cols()):
        copy.wait_send()
    for k in range(3):
        all_dealt(k).wait_send()
    for k in range(2):
        all_got(k).wait_send()
    get_in(2)
    make_new(gamma)
    all_got(2).wait_send()


def step(cap, dealt, quick, collective_id, *operands):
    any_space = pl.BlockSpec(memory_space=pl.ANY)
    smem = pl.BlockSpec(memory_space=pltpu.SMEM)
    vmem = pl.BlockSpec(memory_space=pltpu.VMEM)
    block = jax.ShapeDtypeStruct((SLOTS, BS, BS), jnp.float32)
    dma = pltpu.SemaphoreType.DMA
    panel = pltpu.VMEM((3 * SLOTS + 1, BS, BS), jnp.float32)
    own = pltpu.VMEM((SLOTS, BS, BS), jnp.float32)
    slices = pltpu.VMEM((ROWS * dealt, CUT, BS), jnp.float32)
    fetched = pltpu.VMEM((ROWS, cap + SLOTS, CUT, BS), jnp.float32)
    return pl.pallas_call(
        functools.partial(kernel, cap, dealt, quick),
        out_shape=(block, block, jax.ShapeDtypeStruct((1, 1), jnp.float32)),
        in_specs=[any_space] * 4,
        out_specs=(vmem, vmem, smem),
        scratch_shapes=[
            panel,
            panel,
            own,
            own,
            own,
            pltpu.VMEM((3, dealt, BS, BS), jnp.float32),
            slices,
            slices,
            slices,
            pltpu.VMEM((3, ROWS, cap, CUT, BS), jnp.float32),
            fetched,
            fetched,
            fetched,
            own,
            pltpu.VMEM((2, SLOTS, BS, BS), jnp.float32),
            pltpu.VMEM((2, OFF_DIAG, BS, BS), jnp.float32),
            pltpu.VMEM((2 * OFF_DIAG, BS, BS), jnp.float32),
            pltpu.SMEM((3, 1, SLOTS), jnp.int32),
            pltpu.SMEM((3, 1, SLOTS), jnp.int32),
            pltpu.SMEM((WANT_MOST,), jnp.int32),
            pltpu.VMEM((5, 1, BS), jnp.int32),
            pltpu.SMEM((5, 1, BS), jnp.int32),
            pltpu.VMEM((ROWS, 1, BS), jnp.int32),
            pltpu.SMEM((ROWS, 1, BS), jnp.int32),
            pltpu.VMEM((8, BS), jnp.float32),
            pltpu.VMEM((ROWS, 8, BS), jnp.float32),
            pltpu.VMEM((COLS, 8, BS), jnp.float32),
            dma((9,)),
            dma((2, 2)),
            dma((2, 2)),
            dma((3,)),
            dma((3,)),
            dma((3,)),
            dma((3,)),
            dma,
            dma,
            dma,
            dma,
            dma,
            dma,
            dma((2,)),
            dma((2,)),
            dma((2,)),
            dma((2,)),
        ],
        compiler_params=pltpu.CompilerParams(
            collective_id=collective_id, has_side_effects=True, vmem_limit_bytes=60 * 1024 * 1024
        ),
        cost_estimate=pl.CostEstimate(flops=2 * 9 * 4 * SLOTS * BS**3, bytes_accessed=5 * SLOTS * BS * BS, transcendentals=0),
    )(*operands)


def write_kernel(new_in, ew_in, new_ref, ew_ref, sem):
    pairs = ((new_in, new_ref), (ew_in, ew_ref))
    copies = [pltpu.make_async_copy(src, dst, sem.at[k]) for k, (src, dst) in enumerate(pairs)]
    for copy in copies:
        copy.start()
    for copy in copies:
        copy.wait()


def write_out(new, ew):
    any_space = pl.BlockSpec(memory_space=pl.ANY)
    block = jax.ShapeDtypeStruct((SLOTS, BS, BS), jnp.float32)
    return pl.pallas_call(
        write_kernel,
        out_shape=(block, block),
        in_specs=[any_space, any_space],
        out_specs=(any_space, any_space),
        scratch_shapes=[pltpu.SemaphoreType.DMA((2,))],
    )(new, ew)


def shards(density, hamiltonian, block_rows, block_cols, left_index, right_index):
    terms_first = (2, 0, 1)
    operands = (
        density[0], hamiltonian[0],
        jnp.transpose(left_index, terms_first), jnp.transpose(right_index, terms_first),
    )
    new, ew, over = step(WANT_FEW, min(WANT_FEW, SLOTS), True, 0, *operands)
    new, ew = lax.cond(
        over[0, 0] > 0.0,
        lambda new, ew, *operands: tuple(step(WANT_MOST, SLOTS, False, 1, *operands)[:2]),
        lambda new, ew, *operands: (new, ew),
        new, ew, *operands,
    )
    new, ew = write_out(new, ew)
    return new[None], ew[None]


def solution(mesh):
    in_specs = (
        P("row", "col", None, None),
        P("row", "col", None, None),
        P("row", "col"),
        P("row", "col"),
        P("row", "col", None),
        P("row", "col", None),
    )
    out_specs = (P("row", "col", None, None), P("row", "col", None, None))
    return jax.shard_map(shards, mesh=mesh, in_specs=in_specs, out_specs=out_specs, check_vma=False)
```
